32 devices in a mesh: cell: 8 (over z, y), dp: 4 (over x, core).
Axes of the slice: x: 2, y: 2, z: 4, core: 2. Of those that a mesh axis runs over, the one named last changes fastest.
Arguments:
- state: bfloat16 [163840, 128], P(('cell', 'dp')), may hold values from -6 to 6
- cell_coordinate: bfloat16 [3, 163840], P(None, ('cell', 'dp')), may hold values from 0 to 1
- member_predictions: bfloat16 [4, 1024, 128], P('dp', 'cell'), may hold values from -6 to 6
- measured_values: float32 [4, 1024], P('dp', 'cell'), may hold values from -64 to 64
- obs_error_variance: float32 [4, 1024], P('dp', 'cell'), may hold values from 4 to 64
- observation_coordinate: bfloat16 [4, 3, 1024], P('dp', None, 'cell'), may hold values from 0 to 1
- localization_tile_pairs: int32 [32, 4, 2, 256], P(('cell', 'dp')), may hold values from 0 to 39, as said below
- used_pair_count: int32 [32, 4], P(('cell', 'dp')), may hold values from 1 to 256, as said below
Outputs:
- analysis: bfloat16 [163840, 128], P(('cell', 'dp'))
The draws below stay inside these ranges and needn't reach their ends.
Inputs may be any that keep to these rules, and one draw needn't show every extreme that they name: `localization_tile_pairs`: row 0 names a cell tile of the block (below 40), row 1 an observation tile of the batch (below 8); only the first used_pair_count entries count, and a pair may repeat. `used_pair_count`: in every batch some blocks list exactly 256 pairs.
All inputs are finite; a program needn't handle non-finite values.
Results may differ from the reference program's by a relative error of at most 0.011.
Values may be sent and summed in bfloat16 or wider, within the bound.
No kernel may reach another device: no remote copies, remote signals or barrier semaphores. Data moves between devices by JAX's collectives and lax.ppermute only.
A program may use at most 192 MiB of HBM per device.

```python
import math
import jax
import jax.numpy as jnp
from jax import lax

ENSEMBLE_SIZE = 128
CT = 128
OBS_DEV = 128
CELL_DEV = 5120
MAXP = 256
OBS_BATCH_COUNT = 4
BATCH_OBS_COUNT = 1024
OBS_TILES = 8
BLOCKS = 32
CTILES = 40
NCELLS = 163840


def draw_localization_tile_pairs(key, part):
    key = jax.random.fold_in(key, 11)
    first, second = jax.random.split(key)
    cells = jax.random.randint(first, (BLOCKS, OBS_BATCH_COUNT, 1, MAXP), 0, CTILES)
    obs = jax.random.randint(second, (BLOCKS, OBS_BATCH_COUNT, 1, MAXP), 0, OBS_TILES)
    cells = cells.at[0, 0, 0, 0].set(CTILES - 1)
    obs = obs.at[0, 0, 0, 0].set(OBS_TILES - 1)
    return jnp.concatenate([cells, obs], axis=2).astype(jnp.int32)


def draw_used_pair_count(key, part):
    key = jax.random.fold_in(key, 23)
    first, second = jax.random.split(key)
    base = jax.random.randint(first, (BLOCKS, OBS_BATCH_COUNT), max(1, MAXP // 8), MAXP // 2 + 1)
    orders = jax.vmap(lambda batch_position: jax.random.permutation(batch_position, BLOCKS))(jax.random.split(second, OBS_BATCH_COUNT))
    heavy = jnp.transpose(orders < max(1, BLOCKS // 8))
    return jnp.where(heavy, MAXP, base).astype(jnp.int32)


def block_scale(key, extent, shards, least, high):
    level, own = 1.0, jax.random.fold_in(key, 6)
    for position, blocks in shards:
        draws = jnp.exp(jax.random.uniform(jax.random.fold_in(own, position), (blocks,), jnp.float32, least / len(shards), high / len(shards)))
        level = level * jnp.repeat(draws, extent[position] // blocks).reshape([-1 if axis == position else 1 for axis in range(len(extent))])
    return level


def normal_values(own_key, shape, width, bound, cuts=(), kind=jnp.bfloat16):
    loudness = block_scale(own_key, shape, cuts, -0.22, 0.18) if cuts else 1.0
    result = jax.random.normal(own_key, shape, jnp.float32) * width * loudness
    return jnp.minimum(jnp.maximum(result, -bound), bound).astype(kind)


def setup_inputs(seed: int = 0) -> dict:
    streams_of = jax.random.split(jax.random.key(seed), 9)
    state = normal_values(streams_of[0], (NCELLS, ENSEMBLE_SIZE), 1.0, 6.0, ((0, 32),))
    cell_coordinate = jnp.clip(1.0 * jax.random.uniform(streams_of[1], (3, NCELLS), jnp.float32) ** block_scale(streams_of[1], (3, NCELLS), ((1, 32),), -0.2, 0.2), 0.0, 1.0).astype(jnp.bfloat16)
    member_predictions = normal_values(streams_of[2], (OBS_BATCH_COUNT, BATCH_OBS_COUNT, ENSEMBLE_SIZE), 1.0, 6.0, ((0, 4), (1, 8)))
    measured_values = normal_values(streams_of[3], (OBS_BATCH_COUNT, BATCH_OBS_COUNT), 16.0, 64.0, ((0, 4), (1, 8)), jnp.float32)
    obs_error_variance = jnp.clip(jnp.exp(math.log(64.0) - 2.7725887 * jax.random.uniform(streams_of[4], (OBS_BATCH_COUNT, BATCH_OBS_COUNT), jnp.float32) ** block_scale(streams_of[4], (OBS_BATCH_COUNT, BATCH_OBS_COUNT), ((0, 4), (1, 8)), -0.2, 0.2)), 4.0, 64.0)
    observation_coordinate = jnp.clip(1.0 * jax.random.uniform(streams_of[5], (OBS_BATCH_COUNT, 3, BATCH_OBS_COUNT), jnp.float32) ** block_scale(streams_of[5], (OBS_BATCH_COUNT, 3, BATCH_OBS_COUNT), ((0, 4), (2, 8)), -0.2, 0.2), 0.0, 1.0).astype(jnp.bfloat16)
    localization_tile_pairs = draw_localization_tile_pairs(jax.random.fold_in(streams_of[8], 71), 0)
    used_pair_count = draw_used_pair_count(jax.random.fold_in(streams_of[8], 71), 0)
    return dict(state=state, cell_coordinate=cell_coordinate, member_predictions=member_predictions, measured_values=measured_values, obs_error_variance=obs_error_variance, observation_coordinate=observation_coordinate, localization_tile_pairs=localization_tile_pairs, used_pair_count=used_pair_count)


taper_rate = 2.0

def taper(cell_places, obs_places):
    diff = cell_places[:, :, None].astype(jnp.float32) - obs_places[:, None, :].astype(jnp.float32)
    return jnp.exp(-taper_rate * jnp.sum(diff * diff, axis=0))

def tile_term(gain, cell_places, spread, member_pull, obs_places, cell_tile, obs_tile):
    start_c = (cell_tile * CT).astype(jnp.int32)
    start_o = (obs_tile * OBS_DEV).astype(jnp.int32)
    rows = lax.dynamic_slice_in_dim(gain, start_c, CT, 0)
    places = lax.dynamic_slice_in_dim(cell_places, start_c, CT, 1)
    obs_rows = lax.dynamic_slice_in_dim(spread, start_o, OBS_DEV, 0)
    pull_rows = lax.dynamic_slice_in_dim(member_pull, start_o, OBS_DEV, 0)
    obs_here = lax.dynamic_slice_in_dim(obs_places, start_o, OBS_DEV, 1)
    score = lax.dot_general(rows.astype(jnp.float32), obs_rows.astype(jnp.float32), (((1,), (1,)), ((), ())), preferred_element_type=jnp.float32)
    weights = (taper(places, obs_here) * score).astype(jnp.bfloat16)
    return jnp.dot(weights.astype(jnp.float32), pull_rows.astype(jnp.float32), preferred_element_type=jnp.float32)

def reference(state, cell_coordinate, member_predictions, measured_values, obs_error_variance, observation_coordinate, localization_tile_pairs, used_pair_count):
    top_precision = lax.Precision.HIGHEST
    eye = jnp.eye(ENSEMBLE_SIZE, dtype=jnp.float32)
    running_total = eye
    batch_data = []
    for batch_position in range(OBS_BATCH_COUNT):
        present_state = jnp.dot(member_predictions[batch_position].astype(jnp.float32), running_total, precision=top_precision)
        obs_mean = jnp.mean(present_state, axis=1, keepdims=True)
        spread = present_state - obs_mean
        innovation = measured_values[batch_position] - obs_mean[:, 0]
        inv_var = 1.0 / obs_error_variance[batch_position]
        cross = jnp.dot(spread.T, spread * inv_var[:, None], precision=top_precision) / (ENSEMBLE_SIZE - 1)
        pull = jnp.dot(spread.T, inv_var * innovation, precision=top_precision) / (ENSEMBLE_SIZE - 1)
        chol = jnp.linalg.cholesky(eye + cross)
        inverse = jax.scipy.linalg.cho_solve((chol, True), eye)
        change = jnp.dot(inverse, pull[:, None] - 0.5 * cross, precision=top_precision)
        transform = eye + change - jnp.mean(change, axis=0, keepdims=True)
        running_total = jnp.dot(running_total, transform, precision=top_precision)
        member_pull = (inv_var[:, None] * (innovation[:, None] - 0.5 * spread)).astype(jnp.bfloat16)
        batch_data.append((spread.astype(jnp.bfloat16), member_pull, observation_coordinate[batch_position], inverse / (ENSEMBLE_SIZE - 1)))
    work = state.astype(jnp.float32).reshape(BLOCKS, CELL_DEV, ENSEMBLE_SIZE)
    places_all = jnp.transpose(cell_coordinate.reshape(3, BLOCKS, CELL_DEV), (1, 0, 2))
    for batch_position in range(OBS_BATCH_COUNT):
        spread_k, pull_k, places_k, inverse_k = batch_data[batch_position]

        def update_block(items):
            block, places, pairs, count = items
            perturbation = block - jnp.mean(block, axis=1, keepdims=True)
            gain = jnp.dot(perturbation, inverse_k, precision=top_precision).astype(jnp.bfloat16)

            def add_pair(i, delta):
                term = tile_term(gain, places, spread_k, pull_k, places_k, pairs[0, i], pairs[1, i])
                start_c = (pairs[0, i] * CT).astype(jnp.int32)
                old = lax.dynamic_slice_in_dim(delta, start_c, CT, 0)
                return lax.dynamic_update_slice_in_dim(delta, old + term, start_c, 0)
            delta = lax.fori_loop(jnp.int32(0), count.astype(jnp.int32), add_pair, jnp.zeros((CELL_DEV, ENSEMBLE_SIZE), jnp.float32))
            return block + delta
        work = lax.map(update_block, (work, places_all, localization_tile_pairs[:, batch_position], used_pair_count[:, batch_position]))
    return work.reshape(NCELLS, ENSEMBLE_SIZE).astype(jnp.bfloat16)
```

```python
import functools
import math

import jax
import jax.numpy as jnp
from jax import lax
from jax.experimental import pallas as pl
from jax.experimental.pallas import tpu as pltpu
from jax.sharding import PartitionSpec as P

CT = 128
OBS_DEV = 128
EXTRA = 16
taper_rate = 2.0
LOG2E = math.log2(math.e)
TOP = lax.Precision.HIGHEST
GROUP = 4
F32 = jnp.float32
BF16 = jnp.bfloat16
VMEM_LIMIT = 56 * 1024 * 1024


def in_vmem():
    return pl.BlockSpec(memory_space=pltpu.VMEM)


def in_smem():
    return pl.BlockSpec(memory_space=pltpu.SMEM)


def split3(x):
    hi = x.astype(BF16).astype(F32)
    mid = (x - hi).astype(BF16).astype(F32)
    return hi, mid, x - hi - mid


def split2(x):
    hi = x.astype(BF16)
    return hi, (x - hi.astype(F32)).astype(BF16)


def mm(a, b):
    return jnp.dot(a, b, precision=TOP, preferred_element_type=F32)


def mm16(a, b):
    return jnp.dot(a, b, preferred_element_type=F32)


def pack_kernel(pred, value, variance, coord, out):
    members = pred.shape[1]
    out[:members, :] = pred[...].astype(F32).T.astype(BF16)
    rows = lax.broadcasted_iota(jnp.int32, (EXTRA, OBS_DEV), 0)
    lines = split3(value[...]) + split3(variance[...])
    place = coord[...].astype(F32)
    lines = lines + tuple(place[j : j + 1] for j in range(3))
    extra = jnp.zeros((EXTRA, OBS_DEV), F32)
    for j, line in enumerate(lines):
        extra = jnp.where(rows == j, line, extra)
    out[members:, :] = extra.astype(BF16)


def pack(pred, value, variance, coord):
    return pl.pallas_call(
        pack_kernel,
        out_shape=jax.ShapeDtypeStruct((pred.shape[1] + EXTRA, pred.shape[0]), BF16),
        in_specs=[in_vmem()] * 4,
        out_specs=in_vmem(),
        name="pack_observations",
    )(pred, value, variance, coord)


def inverse_of(eye, s, both):
    n = s.shape[0]
    bound = jnp.max(jnp.sum(jnp.abs(s), axis=0, keepdims=True))
    scale = 2.0 / (2.0 + bound)
    both[:n] = eye - scale * (eye + s)
    both[n:] = eye

    def more(carry):
        rho, left = carry
        return (rho > 1e-8) & (left > 0)

    def factor(carry):
        rho, left = carry
        new = mm(both[...], both[:n])
        both[:n] = new[:n]
        both[n:] += new[n:]
        return rho * rho, left - 1

    lax.while_loop(more, factor, (bound / (2.0 + bound), jnp.int32(40)))
    return scale * both[n:]


def chain_kernel(blocks, identity, bt_out, mp_out, oc_out, yhl, wz, gs, us, both_ref):
    tiles, batches = blocks.shape[0], blocks.shape[1]
    members = blocks.shape[2] - EXTRA
    count = tiles * OBS_DEV
    eye = identity[...]

    for k in range(batches):
        g = jnp.zeros((members + 8, members), F32)
        for u in range(tiles):
            y = blocks[u, k, :members, :].astype(F32)
            e = blocks[u, k, members:, :].astype(F32)
            value = e[0:1] + e[1:2] + e[2:3]
            variance = e[3:4] + e[4:5] + e[5:6]
            place = e[6:9]
            mean = jnp.mean(y, axis=0, keepdims=True)
            yc = y - mean
            w = 1.0 / variance
            z = (value - mean) * w
            ew = jnp.exp(-taper_rate * jnp.sum(place * place, axis=0, keepdims=True))
            where = pl.ds(u * OBS_DEV, OBS_DEV)
            hi, lo = split2(yc)
            yhl[k, :members, where] = hi
            yhl[k, members:, where] = lo
            wz[k, 0:1, where] = w
            wz[k, 1:2, where] = z
            wz[k, 2:3, where] = ew * (1.0 / (members - 1))
            oc_out[k, u] = jnp.concatenate([place * (2 * taper_rate * LOG2E), jnp.zeros((5, OBS_DEV), F32)], axis=0)
            left = jnp.concatenate([yc * w, jnp.broadcast_to(z, (8, OBS_DEV))], axis=0)
            g = g + lax.dot_general(left, yc, (((1,), (1,)), ((), ())), precision=TOP, preferred_element_type=F32)
        gs[k] = g[:members]
        us[k] = g[members:]

    qt = eye - 1.0 / members
    p = jnp.full((8, members), 1.0 / members, F32)
    for k in range(batches):
        g_k = gs[k]
        inverse = inverse_of(eye, g_k * (1.0 / (members - 1)), both_ref)
        step = mm(us[k], inverse) * (1.0 / (members - 1))
        mt = mm(inverse, qt)
        ht = 0.5 * qt + p[0:1]
        hi, lo = split2(jnp.concatenate([mt, ht], axis=0))
        twice = jnp.concatenate([hi, hi], axis=1)
        for u in range(tiles):
            where = pl.ds(u * OBS_DEV, OBS_DEV)
            both = mm16(twice, yhl[k, :, where]) + mm16(lo, yhl[k, :members, where])
            bt_out[k, u] = (both[:members] * wz[k, 2:3, where]).astype(BF16)
            mp_out[k, u] = (wz[k, 1:2, where] - wz[k, 0:1, where] * both[members:]).T.astype(BF16)
        if k + 1 < batches:
            half = 0.5 * (eye + inverse)
            p = p + mm(step, qt)
            qt = 0.5 * (qt + mt)
            for j in range(k + 1, batches):
                g_j = gs[j]
                us[j] = mm(us[j] - mm(step, g_j), half)
                gs[j] = mm(half, mm(g_j, half))


def chain(blocks):
    tiles, batches = blocks.shape[:2]
    members = blocks.shape[2] - EXTRA
    return pl.pallas_call(
        chain_kernel,
        out_shape=(
            jax.ShapeDtypeStruct((batches, tiles, members, OBS_DEV), BF16),
            jax.ShapeDtypeStruct((batches, tiles, OBS_DEV, members), BF16),
            jax.ShapeDtypeStruct((batches, tiles, 8, OBS_DEV), F32),
        ),
        in_specs=[in_vmem()] * 2,
        out_specs=(in_vmem(),) * 3,
        scratch_shapes=[
            pltpu.VMEM((batches, 2 * members, tiles * OBS_DEV), BF16),
            pltpu.VMEM((batches, 8, tiles * OBS_DEV), F32),
            pltpu.VMEM((batches, members, members), F32),
            pltpu.VMEM((batches, 8, members), F32),
            pltpu.VMEM((2 * members, members), F32),
        ],
        compiler_params=pltpu.CompilerParams(vmem_limit_bytes=VMEM_LIMIT),
        name="serial_transforms",
    )(blocks, jnp.eye(members, dtype=F32))


def cell_kernel(codes, mults, sizes, state, coord, select, bt, mp, oc, out, acc, pert, cb, ec):
    batches, obs_tiles = bt.shape[:2]
    members = state.shape[1]
    tiles = state.shape[0] // CT
    def prepare(t, _):
        where = pl.ds(pl.multiple_of(t * CT, CT), CT)
        acc[t] = state[where, :].astype(F32)
        place = lax.dot_general(
            coord[:, where], select[...], (((0,), (0,)), ((), ())), preferred_element_type=F32
        )
        norm = jnp.zeros((CT, members), F32)
        for j in range(3):
            c = place[:, j * members : (j + 1) * members]
            cb[j, t] = c
            norm = norm + c * c
        ec[t] = jnp.exp(-taper_rate * norm)
        return 0

    lax.fori_loop(0, tiles, prepare, 0)
    acc[tiles] = jnp.zeros((CT, members), F32)
    pert[tiles] = jnp.zeros((CT, members), BF16)
    for j in range(3):
        cb[j, tiles] = jnp.zeros((CT, members), F32)

    for k in range(batches):

        def centre(t, _):
            x = acc[t]
            pert[t] = ((x - jnp.mean(x, axis=1, keepdims=True)) * ec[t]).astype(BF16)
            return 0

        lax.fori_loop(0, tiles, centre, 0)

        def several(i, _):
            for j in range(GROUP):
                code = codes[k, i * GROUP + j]
                t, u = code // obs_tiles, code % obs_tiles
                score = mm16(pert[t], bt[k, u]) * mults[k, i * GROUP + j]
                o = oc[k, u]
                x = cb[0, t] * o[0:1] + cb[1, t] * o[1:2] + cb[2, t] * o[2:3]
                weights = (jnp.exp2(x) * score).astype(BF16)
                acc[t] += mm16(weights, mp[k, u])
            return 0

        lax.fori_loop(0, (sizes[k] + GROUP - 1) // GROUP, several, 0)

    def finish(t, _):
        out[pl.ds(pl.multiple_of(t * CT, CT), CT), :] = acc[t].astype(BF16)
        return 0

    lax.fori_loop(0, tiles, finish, 0)


def cells(codes, mults, sizes, state, coord, bt, mp, oc):
    members = state.shape[1]
    select = (jnp.arange(3 * members)[None, :] // members == jnp.arange(16)[:, None]).astype(BF16)
    tiles = state.shape[0] // CT
    return pl.pallas_call(
        cell_kernel,
        out_shape=jax.ShapeDtypeStruct(state.shape, BF16),
        in_specs=[in_smem()] * 3 + [in_vmem()] * 6,
        out_specs=in_vmem(),
        scratch_shapes=[
            pltpu.VMEM((tiles + 1, CT, members), F32),
            pltpu.VMEM((tiles + 1, CT, members), BF16),
            pltpu.VMEM((3, tiles + 1, CT, members), F32),
            pltpu.VMEM((tiles, CT, members), F32),
        ],
        compiler_params=pltpu.CompilerParams(vmem_limit_bytes=VMEM_LIMIT),
        name="cell_updates",
    )(codes, mults, sizes, state, coord, select, bt, mp, oc)


def distinct_pairs(pairs, counts, tiles, obs_tiles):
    slots = pairs.shape[2]
    position = jnp.arange(slots, dtype=jnp.int32)
    valid = position[None, :] < counts[:, None]
    code = jnp.where(valid, pairs[:, 0] * obs_tiles + pairs[:, 1], tiles * obs_tiles)
    same = code[:, :, None] == code[:, None, :]
    times = jnp.sum(same, axis=2, dtype=jnp.int32)
    earlier = position[None, :] < position[:, None]
    first = valid & ~jnp.any(same & earlier[None], axis=2)
    rank = jnp.sum(first[:, None, :] & (code[:, None, :] < code[:, :, None]), axis=2, dtype=jnp.int32)
    slot = jnp.arange(slots + GROUP, dtype=jnp.int32)
    here = first[:, None, :] & (rank[:, None, :] == slot[None, :, None])
    codes = jnp.sum(jnp.where(here, code[:, None, :], 0), axis=2, dtype=jnp.int32)
    mults = jnp.sum(jnp.where(here, times[:, None, :], 0), axis=2, dtype=jnp.int32)
    codes = jnp.where(mults > 0, codes, tiles * obs_tiles)
    sizes = jnp.sum(first, axis=1, dtype=jnp.int32)
    return codes, mults.astype(F32), sizes


def local(
    state,
    cell_coordinate,
    member_predictions,
    measured_values,
    obs_error_variance,
    observation_coordinate,
    localization_tile_pairs,
    used_pair_count,
):
    obs_tiles = lax.axis_size("cell")
    batches = lax.axis_size("dp")
    tiles = state.shape[0] // CT
    mine = pack(member_predictions[0], measured_values, obs_error_variance, observation_coordinate[0])
    blocks = lax.all_gather(mine, ("cell", "dp"), axis=0)
    blocks = blocks.reshape((obs_tiles, batches) + mine.shape)
    codes, mults, sizes = distinct_pairs(localization_tile_pairs[0], used_pair_count[0], tiles, obs_tiles)
    coord = jnp.concatenate([cell_coordinate, jnp.zeros((13, cell_coordinate.shape[1]), BF16)], axis=0)
    bt, mp, oc = chain(blocks)
    return cells(codes, mults, sizes, state, coord, bt, mp, oc)


def solution(mesh):
    placed = (
        P(("cell", "dp"), None),
        P(None, ("cell", "dp")),
        P("dp", "cell", None),
        P("dp", "cell"),
        P("dp", "cell"),
        P("dp", None, "cell"),
        P(("cell", "dp"), None, None, None),
        P(("cell", "dp"), None),
    )
    return jax.shard_map(
        local, mesh=mesh, in_specs=placed, out_specs=P(("cell", "dp"), None), check_vma=False
    )
```

```python
import functools
import math

import jax
import jax.numpy as jnp
from jax import lax
from jax.experimental import pallas as pl
from jax.experimental.pallas import tpu as pltpu
from jax.sharding import PartitionSpec as P

CT = 128
OBS_DEV = 128
EXTRA = 16
taper_rate = 2.0
LOG2E = math.log2(math.e)
TOP = lax.Precision.HIGHEST
GROUP = 4
F32 = jnp.float32
BF16 = jnp.bfloat16
VMEM_LIMIT = 56 * 1024 * 1024


def in_vmem():
    return pl.BlockSpec(memory_space=pltpu.VMEM)


def in_smem():
    return pl.BlockSpec(memory_space=pltpu.SMEM)


def split3(x):
    hi = x.astype(BF16).astype(F32)
    mid = (x - hi).astype(BF16).astype(F32)
    return hi, mid, x - hi - mid


def split2(x):
    hi = x.astype(BF16)
    return hi, (x - hi.astype(F32)).astype(BF16)


def mm(a, b):
    return jnp.dot(a, b, precision=TOP, preferred_element_type=F32)


def mm16(a, b):
    return jnp.dot(a, b, preferred_element_type=F32)


def pack_kernel(pred, value, variance, coord, out):
    members = pred.shape[1]
    out[:members, :] = pred[...].astype(F32).T.astype(BF16)
    rows = lax.broadcasted_iota(jnp.int32, (EXTRA, OBS_DEV), 0)
    lines = split3(value[...]) + split3(variance[...])
    place = coord[...].astype(F32)
    lines = lines + tuple(place[j : j + 1] for j in range(3))
    extra = jnp.zeros((EXTRA, OBS_DEV), F32)
    for j, line in enumerate(lines):
        extra = jnp.where(rows == j, line, extra)
    out[members:, :] = extra.astype(BF16)


def pack(pred, value, variance, coord):
    return pl.pallas_call(
        pack_kernel,
        out_shape=jax.ShapeDtypeStruct((pred.shape[1] + EXTRA, pred.shape[0]), BF16),
        in_specs=[in_vmem()] * 4,
        out_specs=in_vmem(),
        name="pack_observations",
    )(pred, value, variance, coord)


def steps_of(size):
    return size.bit_length() - 1


def relative_place(rc, rd, tiles, batches):
    nc, nd = steps_of(tiles), steps_of(batches)
    place = 0
    for s in range(nc):
        place |= ((rc >> (nc - 1 - s)) & 1) << s
    for s in range(nd):
        place |= ((rd >> (nd - 1 - s)) & 1) << (nc + s)
    return place


def swapped(block, axis, mask):
    return lax.ppermute(block, axis, [(i, i ^ mask) for i in range(lax.axis_size(axis))])


def gathered(mine):
    near = mine[None]
    moves = [("cell", 1 << b) for b in reversed(range(steps_of(lax.axis_size("cell"))))]
    moves += [("dp", 1 << b) for b in reversed(range(steps_of(lax.axis_size("dp"))))]
    for n, (axis, mask) in enumerate(moves):
        far = swapped(near, axis, mask)
        if n + 1 < len(moves):
            near = jnp.concatenate([near, far], axis=0)
    return near, far


def inverse_of(eye, s, both):
    n = s.shape[0]
    bound = jnp.max(jnp.sum(jnp.abs(s), axis=0, keepdims=True))
    scale = 2.0 / (2.0 + bound)
    both[:n] = eye - scale * (eye + s)
    both[n:] = eye

    def more(carry):
        rho, left = carry
        return (rho > 1e-8) & (left > 0)

    def factor(carry):
        rho, left = carry
        new = mm(both[...], both[:n])
        both[:n] = new[:n]
        both[n:] += new[n:]
        return rho * rho, left - 1

    lax.while_loop(more, factor, (bound / (2.0 + bound), jnp.int32(40)))
    return scale * both[n:]


def chain_kernel(near, far, identity, bt_out, mp_out, oc_out, yhl, wz, gs, us, both_ref):
    batches, tiles = bt_out.shape[:2]
    members = near.shape[1] - EXTRA
    eye = identity[...]
    my_tile, my_batch = lax.axis_index("cell"), lax.axis_index("dp")

    for rd in range(batches):
        lefts, ycs = [], []
        k = my_batch ^ rd
        for rc in range(tiles):
            r = relative_place(rc, rd, tiles, batches)
            source, r = (near, r) if r < near.shape[0] else (far, r - near.shape[0])
            u = my_tile ^ rc
            y = source[r, :members, :].astype(F32)
            e = source[r, members:, :].astype(F32)
            value = e[0:1] + e[1:2] + e[2:3]
            variance = e[3:4] + e[4:5] + e[5:6]
            place = e[6:9]
            mean = jnp.mean(y, axis=0, keepdims=True)
            yc = y - mean
            w = 1.0 / variance
            z = (value - mean) * w
            ew = jnp.exp(-taper_rate * jnp.sum(place * place, axis=0, keepdims=True))
            where = pl.ds(pl.multiple_of(u * OBS_DEV, OBS_DEV), OBS_DEV)
            hi, lo = split2(yc)
            yhl[k, :members, where] = hi
            yhl[k, members:, where] = lo
            wz[k, 0:1, where] = w
            wz[k, 1:2, where] = z
            wz[k, 2:3, where] = ew * (1.0 / (members - 1))
            oc_out[k, u] = jnp.concatenate([place * (2 * taper_rate * LOG2E), jnp.zeros((5, OBS_DEV), F32)], axis=0)
            lefts.append(jnp.concatenate([yc * w, jnp.broadcast_to(z, (8, OBS_DEV))], axis=0))
            ycs.append(yc)
        g = lax.dot_general(
            jnp.concatenate(lefts, axis=1), jnp.concatenate(ycs, axis=1), (((1,), (1,)), ((), ())),
            precision=TOP, preferred_element_type=F32,
        )
        gs[k] = g[:members]
        us[k] = g[members:]

    qt = eye - 1.0 / members
    p = jnp.full((8, members), 1.0 / members, F32)
    for k in range(batches):
        g_k = gs[k]
        inverse = inverse_of(eye, g_k * (1.0 / (members - 1)), both_ref)
        step = mm(us[k], inverse) * (1.0 / (members - 1))
        mt = mm(inverse, qt)
        ht = 0.5 * qt + p[0:1]
        hi, lo = split2(jnp.concatenate([mt, ht], axis=0))
        twice = jnp.concatenate([hi, hi], axis=1)
        for u in range(tiles):
            where = pl.ds(u * OBS_DEV, OBS_DEV)
            both = mm16(twice, yhl[k, :, where]) + mm16(lo, yhl[k, :members, where])
            bt_out[k, u] = (both[:members] * wz[k, 2:3, where]).astype(BF16)
            mp_out[k, u] = (wz[k, 1:2, where] - wz[k, 0:1, where] * both[members:]).T.astype(BF16)
        if k + 1 < batches:
            half = 0.5 * (eye + inverse)
            p = p + mm(step, qt)
            qt = 0.5 * (qt + mt)
            for j in range(k + 1, batches):
                g_j = gs[j]
                us[j] = mm(us[j] - mm(step, g_j), half)
                gs[j] = mm(half, mm(g_j, half))


def chain(near, far, tiles, batches):
    members = near.shape[1] - EXTRA
    return pl.pallas_call(
        chain_kernel,
        out_shape=(
            jax.ShapeDtypeStruct((batches, tiles, members, OBS_DEV), BF16),
            jax.ShapeDtypeStruct((batches, tiles, OBS_DEV, members), BF16),
            jax.ShapeDtypeStruct((batches, tiles, 8, OBS_DEV), F32),
        ),
        in_specs=[in_vmem()] * 3,
        out_specs=(in_vmem(),) * 3,
        scratch_shapes=[
            pltpu.VMEM((batches, 2 * members, tiles * OBS_DEV), BF16),
            pltpu.VMEM((batches, 8, tiles * OBS_DEV), F32),
            pltpu.VMEM((batches, members, members), F32),
            pltpu.VMEM((batches, 8, members), F32),
            pltpu.VMEM((2 * members, members), F32),
        ],
        compiler_params=pltpu.CompilerParams(vmem_limit_bytes=VMEM_LIMIT),
        name="serial_transforms",
    )(near, far, jnp.eye(members, dtype=F32))


def list_kernel(sizes_in, row_codes, col_codes, entries, others, sizes, *, tiles, obs_tiles):
    batches, slots = row_codes.shape
    length = entries.shape[1]
    line = lax.broadcasted_iota(jnp.int32, (slots, slots), 1)
    down = lax.broadcasted_iota(jnp.int32, (slots, slots), 0)
    slot = lax.broadcasted_iota(jnp.int32, (slots, length), 1) - GROUP

    def ones(mask, axis):
        return jnp.sum(jnp.where(mask, 1, 0), axis=axis, keepdims=True)

    for k in range(batches):
        used = sizes_in[k]
        row = row_codes[k : k + 1, :]
        col = col_codes[:, k : k + 1]
        row = jnp.where(line[:1] < used, row, tiles * obs_tiles)
        col = jnp.where(down[:, :1] < used, col, tiles * obs_tiles)
        row_t, col_t = row // obs_tiles, col // obs_tiles
        same = row == col
        times = ones(same, 1)
        first_row = (ones(same & (down < line), 0) == 0) & (row_t < tiles)
        first_col = (ones(same & (line < down), 1) == 0) & (col_t < tiles)
        mates = row_t == col_t
        even_row = (ones(first_col & mates & (col < row), 0) & 1) == 0
        even_col = (ones(first_row & mates & (row < col), 1) & 1) == 0
        place = ones(first_row & even_row & (row <= col), 1) - 1
        here = first_col & (place == slot)
        value = ((col - col_t * obs_tiles) << 10) + times
        size = ones(first_row & even_row, 1)
        entry = jnp.sum(jnp.where(here & even_col, value + (col_t << 16), 0), axis=0, keepdims=True)
        other = jnp.sum(jnp.where(here & ~even_col, value, 0), axis=0, keepdims=True)
        entries[k : k + 1, :] = jnp.where(entry > 0, entry, tiles << 16)
        others[k : k + 1, :] = other
        sizes[k : k + 1, :] = jnp.broadcast_to(size, (1, 128))


def pair_lists(pairs, counts, tiles, obs_tiles):
    batches, slots = pairs.shape[0], pairs.shape[2]
    codes = pairs[:, 0] * obs_tiles + pairs[:, 1]
    length = -(-(slots + 3 * GROUP) // 128) * 128
    entries, others, sizes = pl.pallas_call(
        functools.partial(list_kernel, tiles=tiles, obs_tiles=obs_tiles),
        out_shape=(
            jax.ShapeDtypeStruct((batches, length), jnp.int32),
            jax.ShapeDtypeStruct((batches, length), jnp.int32),
            jax.ShapeDtypeStruct((batches, 128), jnp.int32),
        ),
        in_specs=[in_smem(), in_vmem(), in_vmem()],
        out_specs=(in_vmem(),) * 3,
        name="pair_lists",
    )(counts, codes, codes.T)
    return entries, others, sizes[:, 0]


def cell_kernel(entries, others, sizes, state, coord, select, bt, mp, oc, out, acc, pert, cb, ec, held):
    batches, obs_tiles = bt.shape[:2]
    members = state.shape[1]
    tiles = state.shape[0] // CT
    several = 4 if tiles % 4 == 0 else 1

    def over_tiles(body):
        def some(i, _):
            for j in range(several):
                body(i * several + j)
            return 0

        lax.fori_loop(0, tiles // several, some, 0)

    def prepare(t):
        where = pl.ds(pl.multiple_of(t * CT, CT), CT)
        acc[t] = state[where, :].astype(F32)
        place = lax.dot_general(
            coord[:, where], select[...], (((0,), (0,)), ((), ())), preferred_element_type=F32
        )
        norm = jnp.zeros((CT, members), F32)
        for j in range(3):
            c = place[:, j * members : (j + 1) * members]
            cb[j, t] = c
            norm = norm + c * c
        ec[t] = jnp.exp(-taper_rate * norm)

    over_tiles(prepare)
    acc[tiles] = jnp.zeros((CT, members), F32)
    pert[tiles] = jnp.zeros((CT, members), BF16)
    held[...] = jnp.zeros(held.shape, BF16)
    for j in range(3):
        cb[j, tiles] = jnp.zeros((CT, members), F32)

    for k in range(batches):

        def centre(t):
            x = acc[t]
            pert[t] = ((x - jnp.mean(x, axis=1, keepdims=True)) * ec[t]).astype(BF16)

        over_tiles(centre)

        def named(i, j):
            e, o = entries[k, i * GROUP + j], others[k, i * GROUP + j]
            return e >> 16, (e >> 10) & 63, o >> 10, e & 1023, o & 1023

        def group(i, _):
            terms = []
            for j in range(GROUP):
                t, u0, u1, _, _ = named(i, j)
                terms.append((t, mm16(held[j], jnp.concatenate([mp[k, u0], mp[k, u1]], axis=0))))
            fresh = []
            for j in range(GROUP):
                t, u0, u1, m0, m1 = named(i + 1, j)
                score = mm16(pert[t], jnp.concatenate([bt[k, u0], bt[k, u1]], axis=1))
                halves = []
                for n, (u, m) in enumerate(((u0, m0), (u1, m1))):
                    o = oc[k, u]
                    x = cb[0, t] * o[0:1] + cb[1, t] * o[1:2] + cb[2, t] * o[2:3]
                    halves.append((jnp.exp2(x) * (score[:, n * OBS_DEV : (n + 1) * OBS_DEV] * m.astype(F32))).astype(BF16))
                fresh.append(halves)
            for t, term in terms:
                acc[t] += term
            for j in range(GROUP):
                held[j, :, :OBS_DEV] = fresh[j][0]
                held[j, :, OBS_DEV:] = fresh[j][1]
            return 0

        lax.fori_loop(0, (sizes[k] + GROUP - 1) // GROUP + 1, group, 0)

    def finish(t):
        out[pl.ds(pl.multiple_of(t * CT, CT), CT), :] = acc[t].astype(BF16)

    over_tiles(finish)


def cells(entries, others, sizes, state, coord, bt, mp, oc):
    members = state.shape[1]
    tiles = state.shape[0] // CT
    select = (jnp.arange(3 * members)[None, :] // members == jnp.arange(16)[:, None]).astype(BF16)
    return pl.pallas_call(
        cell_kernel,
        out_shape=jax.ShapeDtypeStruct(state.shape, BF16),
        in_specs=[in_smem()] * 3 + [in_vmem()] * 6,
        out_specs=in_vmem(),
        scratch_shapes=[
            pltpu.VMEM((tiles + 1, CT, members), F32),
            pltpu.VMEM((tiles + 1, CT, members), BF16),
            pltpu.VMEM((3, tiles + 1, CT, members), F32),
            pltpu.VMEM((tiles, CT, members), F32),
            pltpu.VMEM((GROUP, CT, 2 * OBS_DEV), BF16),
        ],
        compiler_params=pltpu.CompilerParams(vmem_limit_bytes=VMEM_LIMIT),
        name="cell_updates",
    )(entries, others, sizes, state, coord, select, bt, mp, oc)


def local(
    state,
    cell_coordinate,
    member_predictions,
    measured_values,
    obs_error_variance,
    observation_coordinate,
    localization_tile_pairs,
    used_pair_count,
):
    obs_tiles = lax.axis_size("cell")
    batches = lax.axis_size("dp")
    tiles = state.shape[0] // CT
    mine = pack(member_predictions[0], measured_values, obs_error_variance, observation_coordinate[0])
    entries, others, sizes = pair_lists(localization_tile_pairs[0], used_pair_count[0], tiles, obs_tiles)
    near, far = gathered(mine)
    coord = jnp.concatenate([cell_coordinate, jnp.zeros((13, cell_coordinate.shape[1]), BF16)], axis=0)
    bt, mp, oc = chain(near, far, obs_tiles, batches)
    return cells(entries, others, sizes, state, coord, bt, mp, oc)


def solution(mesh):
    placed = (
        P(("cell", "dp"), None),
        P(None, ("cell", "dp")),
        P("dp", "cell", None),
        P("dp", "cell"),
        P("dp", "cell"),
        P("dp", None, "cell"),
        P(("cell", "dp"), None, None, None),
        P(("cell", "dp"), None),
    )
    return jax.shard_map(
        local, mesh=mesh, in_specs=placed, out_specs=P(("cell", "dp"), None), check_vma=False
    )
```

```python
import functools
import math

import jax
import jax.numpy as jnp
from jax import lax
from jax.experimental import pallas as pl
from jax.experimental.pallas import tpu as pltpu
from jax.sharding import PartitionSpec as P

CT = 128
OBS_DEV = 128
EXTRA = 16
taper_rate = 2.0
LOG2E = math.log2(math.e)
GROUP = 8
F32 = jnp.float32
BF16 = jnp.bfloat16
VMEM_LIMIT = 56 * 1024 * 1024


def in_vmem():
    return pl.BlockSpec(memory_space=pltpu.VMEM)


def in_smem():
    return pl.BlockSpec(memory_space=pltpu.SMEM)


def parts(x):
    hi = x.astype(BF16)
    rest = x - hi.astype(F32)
    mid = rest.astype(BF16)
    return hi, mid, (rest - mid.astype(F32)).astype(BF16)


def mm16(a, b):
    return jnp.dot(a, b, preferred_element_type=F32)


def mm_parts(a, b):
    left = jnp.concatenate([a[0], a[0], a[1], a[0], a[1], a[2]], axis=1)
    right = jnp.concatenate([b[0], b[1], b[0], b[2], b[1], b[0]], axis=0)
    return mm16(left, right)


def mm(a, b):
    return mm_parts(parts(a), parts(b))


def pack_kernel(pred, value, variance, coord, out):
    members = pred.shape[1]
    out[:members, :] = pred[...].astype(F32).T.astype(BF16)
    rows = lax.broadcasted_iota(jnp.int32, (EXTRA, OBS_DEV), 0)
    lines = tuple(part.astype(F32) for part in parts(value[...]) + parts(variance[...]))
    place = coord[...].astype(F32)
    lines = lines + tuple(place[j : j + 1] for j in range(3))
    extra = jnp.zeros((EXTRA, OBS_DEV), F32)
    for j, line in enumerate(lines):
        extra = jnp.where(rows == j, line, extra)
    out[members:, :] = extra.astype(BF16)


def pack(pred, value, variance, coord):
    return pl.pallas_call(
        pack_kernel,
        out_shape=jax.ShapeDtypeStruct((pred.shape[1] + EXTRA, pred.shape[0]), BF16),
        in_specs=[in_vmem()] * 4,
        out_specs=in_vmem(),
        name="pack_observations",
    )(pred, value, variance, coord)


def steps_of(size):
    return size.bit_length() - 1


def relative_place(rc, rd, tiles, batches):
    nc, nd = steps_of(tiles), steps_of(batches)
    place = 0
    for s in range(nc):
        place |= ((rc >> (nc - 1 - s)) & 1) << s
    for s in range(nd):
        place |= ((rd >> (nd - 1 - s)) & 1) << (nc + s)
    return place


def swapped(block, axis, mask):
    return lax.ppermute(block, axis, [(i, i ^ mask) for i in range(lax.axis_size(axis))])


def gathered(mine, meanwhile):
    near = mine[None]
    moves = [("cell", 1 << b) for b in reversed(range(steps_of(lax.axis_size("cell"))))]
    moves += [("dp", 1 << b) for b in reversed(range(steps_of(lax.axis_size("dp"))))]
    for axis, mask in moves[:-2]:
        near = jnp.concatenate([near, swapped(near, axis, mask)], axis=0)
    near, work = meanwhile(near)
    far = swapped(near, *moves[-2])
    near_other = swapped(near, *moves[-1])
    far, work = lax.optimization_barrier((far, work))
    return (near, far, near_other, swapped(far, *moves[-1])), work


def inverse_of(eye, s, both):
    n = s.shape[0]
    bound = jnp.max(jnp.sum(jnp.abs(s), axis=0, keepdims=True))
    scale = 2.0 / (2.0 + bound)
    rho = bound / (2.0 + bound)
    r = eye - scale * (eye + s)
    both[:n] = mm(r, r)
    both[n:] = eye + r

    def more(carry):
        rho, left = carry
        return (rho > 1e-8) & (left > 0)

    def factor(carry):
        rho, left = carry
        pieces = parts(both[...])
        new = mm_parts(pieces, [p[:n] for p in pieces])
        both[:n] = new[:n]
        both[n:] += new[n:]
        return rho * rho, left - 1

    lax.while_loop(more, factor, (rho * rho, jnp.int32(40)))
    return scale * both[n:]


def chain_kernel(*refs):
    pieces, (bt_out, mp_out, oc_out, ys, wd, gs, us, both_ref) = refs[:4], refs[4:]
    batches, tiles = bt_out.shape[:2]
    members = bt_out.shape[2]
    rows = lax.broadcasted_iota(jnp.int32, (members, members), 0)
    cols = lax.broadcasted_iota(jnp.int32, (members, members), 1)
    eye = jnp.where(rows == cols, 1.0, 0.0)
    my_tile, my_batch = lax.axis_index("cell"), lax.axis_index("dp")

    for rd in range(batches):
        lefts, rights = [], []
        k = my_batch ^ rd
        for rc in range(tiles):
            r = relative_place(rc, rd, tiles, batches)
            source, r = pieces[r // pieces[0].shape[0]], r % pieces[0].shape[0]
            u = my_tile ^ rc
            raw = source[r, :members, :]
            y = raw.astype(F32)
            e = source[r, members:, :].astype(F32)
            value = e[0:1] + e[1:2] + e[2:3]
            variance = e[3:4] + e[4:5] + e[5:6]
            place = e[6:9]
            mean = jnp.mean(y, axis=0, keepdims=True)
            w = 1.0 / variance
            ew = jnp.exp(-taper_rate * jnp.sum(place * place, axis=0, keepdims=True))
            where = pl.ds(pl.multiple_of(u * OBS_DEV, OBS_DEV), OBS_DEV)
            ys[k, :, where] = raw
            wd[k, 0:1, where] = w
            wd[k, 1:2, where] = value
            wd[k, 2:3, where] = ew * (1.0 / (members - 1))
            oc_out[k, u] = jnp.concatenate([place * (2 * taper_rate * LOG2E), jnp.zeros((5, OBS_DEV), F32)], axis=0)
            z = jnp.broadcast_to((value - mean) * w, (16, OBS_DEV))
            lefts.append(jnp.concatenate(parts(jnp.concatenate([(y - mean) * w, z], axis=0)), axis=0))
            rights.append(raw)
        g = lax.dot_general(
            jnp.concatenate(lefts, axis=1), jnp.concatenate(rights, axis=1), (((1,), (1,)), ((), ())),
            preferred_element_type=F32,
        )
        n = members + 16
        g = g[:n] + g[n : 2 * n] + g[2 * n :]
        g = g - jnp.mean(g, axis=1, keepdims=True)
        gs[k] = g[:members]
        us[k] = g[members:]

    qt = eye - 1.0 / members
    p = jnp.full((16, members), 1.0 / members, F32)
    chunk = min(2, tiles) * OBS_DEV
    for k in range(batches):
        inverse = inverse_of(eye, gs[k] * (1.0 / (members - 1)), both_ref)
        inverse_parts = parts(inverse)
        qt_parts = parts(qt)
        mt = mm_parts(inverse_parts, qt_parts)
        ht = 0.5 * qt + p[0:1]
        hi, mid, lo = parts(jnp.concatenate([mt, ht], axis=0))
        twice = jnp.concatenate([hi, mid], axis=1)
        for n in range(tiles * OBS_DEV // chunk):
            where = pl.ds(n * chunk, chunk)
            y = ys[k, :, where]
            both = mm16(twice, jnp.concatenate([y, y], axis=0)) + mm16(lo, y)
            b = (both[:members] * wd[k, 2:3, where]).astype(BF16)
            pull = wd[k, 0:1, where] * (wd[k, 1:2, where] - both[members:])
            for c in range(chunk // OBS_DEV):
                u = n * (chunk // OBS_DEV) + c
                bt_out[k, u] = b[:, c * OBS_DEV : (c + 1) * OBS_DEV]
                mp_out[k, u] = pull[:, c * OBS_DEV : (c + 1) * OBS_DEV].T.astype(BF16)
        if k + 1 < batches:
            half = parts(0.5 * (eye + inverse))
            step = parts(mm_parts(parts(us[k]), inverse_parts) * (1.0 / (members - 1)))
            p = p + mm_parts(step, qt_parts)
            qt = 0.5 * (qt + mt)
            for j in range(k + 1, batches):
                g_j = parts(gs[j])
                gs[j] = mm_parts(half, parts(mm_parts(g_j, half)))
                us[j] = mm_parts(parts(us[j] - mm_parts(step, g_j)), half)


def chain(pieces, tiles, batches):
    members = pieces[0].shape[1] - EXTRA
    return pl.pallas_call(
        chain_kernel,
        out_shape=(
            jax.ShapeDtypeStruct((batches, tiles, members, OBS_DEV), BF16),
            jax.ShapeDtypeStruct((batches, tiles, OBS_DEV, members), BF16),
            jax.ShapeDtypeStruct((batches, tiles, 8, OBS_DEV), F32),
        ),
        in_specs=[in_vmem()] * 4,
        out_specs=(in_vmem(),) * 3,
        scratch_shapes=[
            pltpu.VMEM((batches, members, tiles * OBS_DEV), BF16),
            pltpu.VMEM((batches, 8, tiles * OBS_DEV), F32),
            pltpu.VMEM((batches, members, members), F32),
            pltpu.VMEM((batches, 16, members), F32),
            pltpu.VMEM((2 * members, members), F32),
        ],
        compiler_params=pltpu.CompilerParams(vmem_limit_bytes=VMEM_LIMIT),
        name="serial_transforms",
    )(*pieces)


def list_kernel(sizes_in, pairs, entries, others, *, tiles, obs_tiles):
    batches, _, slots = pairs.shape
    length = entries.shape[1]
    line = lax.broadcasted_iota(jnp.int32, (slots, slots), 1)
    down = lax.broadcasted_iota(jnp.int32, (slots, slots), 0)
    slot = lax.broadcasted_iota(jnp.int32, (slots, length), 1)

    def ones(mask, axis):
        return jnp.sum(jnp.where(mask, 1, 0), axis=axis, keepdims=True)

    row_codes = [pairs[k, 0:1, :] * obs_tiles + pairs[k, 1:2, :] for k in range(batches)]
    row_codes = jnp.concatenate(row_codes + [jnp.zeros((8 - batches, slots), jnp.int32)], axis=0)
    col_codes = row_codes.astype(F32).T.astype(jnp.int32)
    for k in range(batches):
        used = sizes_in[k]
        row = row_codes[k : k + 1]
        col = col_codes[:, k : k + 1]
        row = jnp.where(line[:1] < used, row, tiles * obs_tiles)
        col = jnp.where(down[:, :1] < used, col, tiles * obs_tiles)
        row_t, col_t = row // obs_tiles, col // obs_tiles
        same = row == col
        times = ones(same, 1)
        first_row = (ones(same & (down < line), 0) == 0) & (row_t < tiles)
        first_col = (ones(same & (line < down), 1) == 0) & (col_t < tiles)
        mates = row_t == col_t
        even_row = (ones(first_col & mates & (col < row), 0) & 1) == 0
        even_col = (ones(first_row & mates & (row < col), 1) & 1) == 0
        place = ones(first_row & even_row & (row <= col), 1) - 1
        here = first_col & (place == slot)
        value = ((col - col_t * obs_tiles) << 10) + times
        size = ones(first_row & even_row, 1)
        entry = jnp.sum(jnp.where(here & even_col, value + (col_t << 16), 0), axis=0, keepdims=True)
        other = jnp.sum(jnp.where(here & ~even_col, value, 0), axis=0, keepdims=True)
        entries[k : k + 1, :] = jnp.where(entry > 0, entry, tiles << 16)
        others[k : k + 1, :] = jnp.where(slot[:1] == length - 1, size, other)


def pair_lists(pairs, counts, tiles, obs_tiles):
    batches, slots = pairs.shape[0], pairs.shape[2]
    shape = jax.ShapeDtypeStruct((batches, -(-(slots + GROUP) // 128) * 128), jnp.int32)
    return pl.pallas_call(
        functools.partial(list_kernel, tiles=tiles, obs_tiles=obs_tiles),
        out_shape=(shape, shape),
        in_specs=[in_smem(), in_vmem()],
        out_specs=(in_vmem(),) * 2,
        cost_estimate=pl.CostEstimate(flops=40 * batches * slots * slots, bytes_accessed=16 * batches * slots, transcendentals=0),
        name="pair_lists",
    )(counts, pairs)


def cell_kernel(entries, others, state, coord, bt, mp, oc, out, acc, pert, cb, ec, held, tall):
    batches, obs_tiles = bt.shape[:2]
    members = state.shape[1]
    tiles = state.shape[0] // CT
    several = 4 if tiles % 4 == 0 else 1
    select = jnp.where(
        lax.broadcasted_iota(jnp.int32, (16, 3 * members), 1) // members
        == lax.broadcasted_iota(jnp.int32, (16, 3 * members), 0),
        1.0,
        0.0,
    ).astype(BF16)
    tall[...] = jnp.zeros(tall.shape, F32)
    tall[:3, :] = coord[...].astype(F32)

    def over_tiles(body):
        def some(i, _):
            for j in range(several):
                body(i * several + j)
            return 0

        lax.fori_loop(0, tiles // several, some, 0)

    def prepare(t):
        where = pl.ds(pl.multiple_of(t * CT, CT), CT)
        acc[t] = state[where, :].astype(F32)
        place = lax.dot_general(
            tall[:, where].astype(BF16), select, (((0,), (0,)), ((), ())), preferred_element_type=F32
        )
        norm = jnp.zeros((CT, members), F32)
        for j in range(3):
            c = place[:, j * members : (j + 1) * members]
            cb[j, t] = c
            norm = norm + c * c
        ec[t] = jnp.exp(-taper_rate * norm)

    over_tiles(prepare)
    acc[tiles] = jnp.zeros((CT, members), F32)
    pert[tiles] = jnp.zeros((CT, members), BF16)
    for j in range(3):
        cb[j, tiles] = jnp.zeros((CT, members), F32)

    for k in range(batches):

        def centre(t):
            x = acc[t]
            pert[t] = ((x - jnp.mean(x, axis=1, keepdims=True)) * ec[t]).astype(BF16)

        over_tiles(centre)

        def named(i, j):
            e, o = entries[k, i * GROUP + j], others[k, i * GROUP + j]
            return e >> 16, (e >> 10) & 63, o >> 10, e & 1023, o & 1023

        def weigh(i):
            fresh = []
            for j in range(GROUP):
                t, u0, u1, m0, m1 = named(i, j)
                score = mm16(pert[t], jnp.concatenate([bt[k, u0], bt[k, u1]], axis=1))
                halves = []
                for n, (u, m) in enumerate(((u0, m0), (u1, m1))):
                    o = oc[k, u]
                    x = cb[0, t] * o[0:1] + cb[1, t] * o[1:2] + cb[2, t] * o[2:3]
                    halves.append((jnp.exp2(x) * (score[:, n * OBS_DEV : (n + 1) * OBS_DEV] * m.astype(F32))).astype(BF16))
                fresh.append(halves)
            for j in range(GROUP):
                held[j, :, :OBS_DEV] = fresh[j][0]
                held[j, :, OBS_DEV:] = fresh[j][1]

        def pull(i):
            for j in range(GROUP):
                t, u0, u1, _, _ = named(i, j)
                acc[t] += mm16(held[j], jnp.concatenate([mp[k, u0], mp[k, u1]], axis=0))

        def group(i, _):
            pull(i - 1)
            weigh(i)
            return 0

        groups = (others[k, others.shape[1] - 1] + GROUP - 1) // GROUP
        weigh(0)
        lax.fori_loop(1, groups, group, 0)
        pull(groups - 1)

    def finish(t):
        out[pl.ds(pl.multiple_of(t * CT, CT), CT), :] = acc[t].astype(BF16)

    over_tiles(finish)


def cells(entries, others, state, coord, bt, mp, oc):
    members = state.shape[1]
    tiles = state.shape[0] // CT
    return pl.pallas_call(
        cell_kernel,
        out_shape=jax.ShapeDtypeStruct(state.shape, BF16),
        in_specs=[in_smem()] * 2 + [in_vmem()] * 5,
        out_specs=in_vmem(),
        scratch_shapes=[
            pltpu.VMEM((tiles + 1, CT, members), F32),
            pltpu.VMEM((tiles + 1, CT, members), BF16),
            pltpu.VMEM((3, tiles + 1, CT, members), F32),
            pltpu.VMEM((tiles, CT, members), F32),
            pltpu.VMEM((GROUP, CT, 2 * OBS_DEV), BF16),
            pltpu.VMEM((16, tiles * CT), F32),
        ],
        compiler_params=pltpu.CompilerParams(vmem_limit_bytes=VMEM_LIMIT),
        name="cell_updates",
    )(entries, others, state, coord, bt, mp, oc)


def local(
    state,
    cell_coordinate,
    member_predictions,
    measured_values,
    obs_error_variance,
    observation_coordinate,
    localization_tile_pairs,
    used_pair_count,
):
    obs_tiles = lax.axis_size("cell")
    batches = lax.axis_size("dp")
    tiles = state.shape[0] // CT
    mine = pack(member_predictions[0], measured_values, obs_error_variance, observation_coordinate[0])

    def meanwhile(near):
        near, pairs, counts = lax.optimization_barrier((near, localization_tile_pairs[0], used_pair_count[0]))
        return near, pair_lists(pairs, counts, tiles, obs_tiles)

    pieces, (entries, others) = gathered(mine, meanwhile)
    bt, mp, oc = chain(pieces, obs_tiles, batches)
    return cells(entries, others, state, cell_coordinate, bt, mp, oc)


def solution(mesh):
    placed = (
        P(("cell", "dp"), None),
        P(None, ("cell", "dp")),
        P("dp", "cell", None),
        P("dp", "cell"),
        P("dp", "cell"),
        P("dp", None, "cell"),
        P(("cell", "dp"), None, None, None),
        P(("cell", "dp"), None),
    )
    return jax.shard_map(
        local, mesh=mesh, in_specs=placed, out_specs=P(("cell", "dp"), None), check_vma=False
    )
```

```python
import functools
import math

import jax
import jax.numpy as jnp
from jax import lax
from jax.experimental import pallas as pl
from jax.experimental.pallas import tpu as pltpu
from jax.sharding import PartitionSpec as P

CT = 128
OBS_DEV = 128
EXTRA = 16
taper_rate = 2.0
LOG2E = math.log2(math.e)
GROUP = 8
F32 = jnp.float32
BF16 = jnp.bfloat16
VMEM_LIMIT = 56 * 1024 * 1024


def in_vmem():
    return pl.BlockSpec(memory_space=pltpu.VMEM)


def in_smem():
    return pl.BlockSpec(memory_space=pltpu.SMEM)


def parts(x):
    hi = x.astype(BF16)
    rest = x - hi.astype(F32)
    mid = rest.astype(BF16)
    return hi, mid, (rest - mid.astype(F32)).astype(BF16)


def mm16(a, b):
    return jnp.dot(a, b, preferred_element_type=F32)


def mm_parts(a, b):
    left = jnp.concatenate([a[0], a[0], a[1], a[0], a[1], a[2]], axis=1)
    right = jnp.concatenate([b[0], b[1], b[0], b[2], b[1], b[0]], axis=0)
    return mm16(left, right)


def mm(a, b):
    return mm_parts(parts(a), parts(b))


def pack_kernel(pred, value, variance, coord, out):
    members = pred.shape[1]
    out[:members, :] = pred[...].astype(F32).T.astype(BF16)
    place = coord[...].astype(F32)
    lines = parts(value[...]) + parts(variance[...]) + tuple(place[j : j + 1] for j in range(3))
    out[members:, :] = stacked(lines).astype(BF16)


def pack(pred, value, variance, coord):
    return pl.pallas_call(
        pack_kernel,
        out_shape=jax.ShapeDtypeStruct((pred.shape[1] + EXTRA, pred.shape[0]), BF16),
        in_specs=[in_vmem()] * 4,
        out_specs=in_vmem(),
        name="pack_observations",
    )(pred, value, variance, coord)


def swapped(block, axis, mask):
    return lax.ppermute(block, axis, [(i, i ^ mask) for i in range(lax.axis_size(axis))])


def gathered(mine, meanwhile):
    near = [mine[None]]
    near += [swapped(near[0], "cell", mask) for mask in range(1, lax.axis_size("cell"))]
    near, work = meanwhile(jnp.concatenate(near, axis=0))
    pieces = {0: near}
    mask = lax.axis_size("dp") // 2
    while mask:
        for d in list(pieces):
            pieces[d ^ mask] = swapped(pieces[d], "dp", mask)
        if len(pieces) == 2:
            pieces[mask], work = lax.optimization_barrier((pieces[mask], work))
        mask //= 2
    return [pieces[d] for d in range(len(pieces))], work


def inverse_of(eye, s, both):
    n = s.shape[0]
    bound = jnp.max(jnp.sum(jnp.abs(s), axis=0, keepdims=True))
    scale = 2.0 / (2.0 + bound)
    rho = bound / (2.0 + bound)
    both[:n] = eye - scale * (eye + s)

    def advance(rho, square, total):
        by = 1.0 / (2.0 - rho * rho)
        both[:n] = (2.0 * by) * square - (rho * rho * by) * eye
        both[n:] = (2.0 * by) * total
        return rho * rho * by

    r = both[:n]
    rho = advance(rho, mm(r, r), eye + r)

    def more(carry):
        rho, left = carry
        return (rho > 1e-8) & (left > 0)

    def factor(carry):
        rho, left = carry
        old = both[...]
        pieces = parts(old)
        new = mm_parts(pieces, [p[:n] for p in pieces])
        return advance(rho, new[:n], old[n:] + new[n:]), left - 1

    lax.while_loop(more, factor, (rho, jnp.int32(40)))
    return scale * both[n:]


def stacked(lines):
    width = lines[0].shape[1]
    rows = lax.broadcasted_iota(jnp.int32, (16, width), 0)
    out = jnp.zeros((16, width), F32)
    for j, line in enumerate(lines):
        out = jnp.where(rows == j, line.astype(F32), out)
    return out


def norm_parts(place):
    return parts(-taper_rate * LOG2E * jnp.sum(place * place, axis=0, keepdims=True))


def cell_features(place):
    ones = [jnp.ones((1, place.shape[1]), F32)] * 3
    return stacked([place[j : j + 1] for j in range(3)] * 3 + list(norm_parts(place)) + ones)


def obs_features(place):
    ones = [jnp.ones((1, place.shape[1]), F32)] * 3
    scaled = parts(place * (2 * taper_rate * LOG2E))
    lines = [part[j : j + 1].astype(F32) for part in scaled for j in range(3)]
    return stacked(lines + ones + list(norm_parts(place))).astype(BF16)


def chain_kernel(*refs):
    pieces, (bt_out, mp_out, of_out, ys, wd, gs, us, both_ref) = refs[:-8], refs[-8:]
    batches, tiles = bt_out.shape[:2]
    members = bt_out.shape[2]
    rows = lax.broadcasted_iota(jnp.int32, (members, members), 0)
    cols = lax.broadcasted_iota(jnp.int32, (members, members), 1)
    eye = jnp.where(rows == cols, 1.0, 0.0)
    my_tile, my_batch = lax.axis_index("cell"), lax.axis_index("dp")

    for rd in range(batches):
        lefts, rights = [], []
        k = my_batch ^ rd
        for rc in range(tiles):
            u = my_tile ^ rc
            raw = pieces[rd][rc, :members, :]
            y = raw.astype(F32)
            e = pieces[rd][rc, members:, :].astype(F32)
            value = e[0:1] + e[1:2] + e[2:3]
            variance = e[3:4] + e[4:5] + e[5:6]
            place = e[6:9]
            mean = jnp.mean(y, axis=0, keepdims=True)
            w = 1.0 / variance
            where = pl.ds(pl.multiple_of(u * OBS_DEV, OBS_DEV), OBS_DEV)
            ys[k, :, where] = raw
            wd[k, 0:1, where] = w
            wd[k, 1:2, where] = value
            of_out[k, u] = obs_features(place)
            z = jnp.broadcast_to((value - mean) * w, (16, OBS_DEV))
            lefts.append(jnp.concatenate(parts(jnp.concatenate([(y - mean) * w, z], axis=0)), axis=0))
            rights.append(raw)
        g = lax.dot_general(
            jnp.concatenate(lefts, axis=1), jnp.concatenate(rights, axis=1), (((1,), (1,)), ((), ())),
            preferred_element_type=F32,
        )
        n = members + 16
        g = g[:n] + g[n : 2 * n] + g[2 * n :]
        g = g - jnp.mean(g, axis=1, keepdims=True)
        gs[k] = g[:members]
        us[k] = g[members:]

    qt = eye - 1.0 / members
    p = jnp.full((16, members), 1.0 / members, F32)
    chunk = min(2, tiles) * OBS_DEV
    for k in range(batches):
        inverse = inverse_of(eye, gs[k] * (1.0 / (members - 1)), both_ref)
        inverse_parts = parts(inverse)
        qt_parts = parts(qt)
        mt = mm_parts(inverse_parts, qt_parts)
        ht = 0.5 * qt + p[0:1]
        hi, mid, lo = parts(jnp.concatenate([mt, ht], axis=0))
        twice = jnp.concatenate([hi, mid], axis=1)
        for n in range(tiles * OBS_DEV // chunk):
            where = pl.ds(n * chunk, chunk)
            y = ys[k, :, where]
            both = mm16(twice, jnp.concatenate([y, y], axis=0)) + mm16(lo, y)
            b = (both[:members] * (1.0 / (members - 1))).astype(BF16)
            pull = wd[k, 0:1, where] * (wd[k, 1:2, where] - both[members:])
            for c in range(chunk // OBS_DEV):
                u = n * (chunk // OBS_DEV) + c
                bt_out[k, u] = b[:, c * OBS_DEV : (c + 1) * OBS_DEV]
                mp_out[k, u] = pull[:, c * OBS_DEV : (c + 1) * OBS_DEV].T.astype(BF16)
        if k + 1 < batches:
            half = parts(0.5 * (eye + inverse))
            step = parts(mm_parts(parts(us[k]), inverse_parts) * (1.0 / (members - 1)))
            p = p + mm_parts(step, qt_parts)
            qt = 0.5 * (qt + mt)
            for j in range(k + 1, batches):
                g_j = parts(gs[j])
                gs[j] = mm_parts(half, parts(mm_parts(g_j, half)))
                us[j] = mm_parts(parts(us[j] - mm_parts(step, g_j)), half)


def chain(pieces, tiles, batches):
    members = pieces[0].shape[1] - EXTRA
    return pl.pallas_call(
        chain_kernel,
        out_shape=(
            jax.ShapeDtypeStruct((batches, tiles, members, OBS_DEV), BF16),
            jax.ShapeDtypeStruct((batches, tiles, OBS_DEV, members), BF16),
            jax.ShapeDtypeStruct((batches, tiles, 16, OBS_DEV), BF16),
        ),
        in_specs=[in_vmem()] * len(pieces),
        out_specs=(in_vmem(),) * 3,
        scratch_shapes=[
            pltpu.VMEM((batches, members, tiles * OBS_DEV), BF16),
            pltpu.VMEM((batches, 8, tiles * OBS_DEV), F32),
            pltpu.VMEM((batches, members, members), F32),
            pltpu.VMEM((batches, 16, members), F32),
            pltpu.VMEM((2 * members, members), F32),
        ],
        compiler_params=pltpu.CompilerParams(vmem_limit_bytes=VMEM_LIMIT),
        name="serial_transforms",
    )(*pieces)


def list_kernel(sizes_in, pairs, entries, others, *, tiles, obs_tiles):
    batches, _, slots = pairs.shape
    length = entries.shape[1]
    line = lax.broadcasted_iota(jnp.int32, (slots, slots), 1)
    down = lax.broadcasted_iota(jnp.int32, (slots, slots), 0)
    slot = lax.broadcasted_iota(jnp.int32, (slots, length), 1)

    def ones(mask, axis):
        return jnp.sum(jnp.where(mask, 1, 0), axis=axis, keepdims=True)

    row_codes = [pairs[k, 0:1, :] * obs_tiles + pairs[k, 1:2, :] for k in range(batches)]
    row_codes = jnp.concatenate(row_codes + [jnp.zeros((8 - batches, slots), jnp.int32)], axis=0)
    col_codes = row_codes.astype(F32).T.astype(jnp.int32)
    for k in range(batches):
        used = sizes_in[k]
        row = row_codes[k : k + 1]
        col = col_codes[:, k : k + 1]
        row = jnp.where(line[:1] < used, row, tiles * obs_tiles)
        col = jnp.where(down[:, :1] < used, col, tiles * obs_tiles)
        row_t, col_t = row // obs_tiles, col // obs_tiles
        same = row == col
        times = ones(same, 1)
        first_row = (ones(same & (down < line), 0) == 0) & (row_t < tiles)
        first_col = (ones(same & (line < down), 1) == 0) & (col_t < tiles)
        mates = row_t == col_t
        even_row = (ones(first_col & mates & (col < row), 0) & 1) == 0
        even_col = (ones(first_row & mates & (row < col), 1) & 1) == 0
        place = ones(first_row & even_row & (row <= col), 1) - 1
        here = first_col & (place == slot)
        value = ((col - col_t * obs_tiles) << 10) + times
        size = ones(first_row & even_row, 1)
        entry = jnp.sum(jnp.where(here & even_col, value + (col_t << 16), 0), axis=0, keepdims=True)
        other = jnp.sum(jnp.where(here & ~even_col, value, 0), axis=0, keepdims=True)
        entries[k : k + 1, :] = jnp.where(entry > 0, entry, tiles << 16)
        others[k : k + 1, :] = jnp.where(slot[:1] == length - 1, size, other)


def pair_lists(pairs, counts, tiles, obs_tiles):
    batches, slots = pairs.shape[0], pairs.shape[2]
    shape = jax.ShapeDtypeStruct((batches, -(-(slots + GROUP) // 128) * 128), jnp.int32)
    return pl.pallas_call(
        functools.partial(list_kernel, tiles=tiles, obs_tiles=obs_tiles),
        out_shape=(shape, shape),
        in_specs=[in_smem(), in_vmem()],
        out_specs=(in_vmem(),) * 2,
        cost_estimate=pl.CostEstimate(flops=40 * batches * slots * slots, bytes_accessed=16 * batches * slots, transcendentals=0),
        name="pair_lists",
    )(counts, pairs)


def cell_kernel(entries, others, state, coord, bt, mp, of, out, acc, pert, feat, held, tall):
    batches, obs_tiles = bt.shape[:2]
    members = state.shape[1]
    tiles = state.shape[0] // CT
    several = 4 if tiles % 4 == 0 else 1
    tall[...] = cell_features(coord[...].astype(F32))

    def over_tiles(body):
        def some(i, _):
            for j in range(several):
                body(i * several + j)
            return 0

        lax.fori_loop(0, tiles // several, some, 0)

    def prepare(t):
        where = pl.ds(pl.multiple_of(t * CT, CT), CT)
        acc[t] = state[where, :].astype(F32)
        feat[t] = tall[:, where].T.astype(BF16)

    over_tiles(prepare)
    acc[tiles] = jnp.zeros((CT, members), F32)
    pert[tiles] = jnp.zeros((CT, members), BF16)
    feat[tiles] = jnp.zeros((CT, 16), BF16)

    for k in range(batches):

        def centre(t):
            x = acc[t]
            pert[t] = ((x - jnp.mean(x, axis=1, keepdims=True))).astype(BF16)

        over_tiles(centre)

        def named(i, j):
            e, o = entries[k, i * GROUP + j], others[k, i * GROUP + j]
            return e >> 16, (e >> 10) & 63, o >> 10, e & 1023, o & 1023

        def weigh(i):
            for j in range(GROUP):
                t, u0, u1, m0, m1 = named(i, j)
                score = mm16(pert[t], jnp.concatenate([bt[k, u0], bt[k, u1]], axis=1))
                power = mm16(feat[t], jnp.concatenate([of[k, u0], of[k, u1]], axis=1))
                taper = jnp.exp2(power)
                for n, m in enumerate((m0, m1)):
                    cut = slice(n * OBS_DEV, (n + 1) * OBS_DEV)
                    held[j, :, cut] = (taper[:, cut] * (score[:, cut] * m.astype(F32))).astype(BF16)

        def pull(i):
            for j in range(GROUP):
                t, u0, u1, _, _ = named(i, j)
                acc[t] += mm16(held[j], jnp.concatenate([mp[k, u0], mp[k, u1]], axis=0))

        def group(i, _):
            pull(i - 1)
            weigh(i)
            return 0

        groups = (others[k, others.shape[1] - 1] + GROUP - 1) // GROUP
        weigh(0)
        lax.fori_loop(1, groups, group, 0)
        pull(groups - 1)

    def finish(t):
        out[pl.ds(pl.multiple_of(t * CT, CT), CT), :] = acc[t].astype(BF16)

    over_tiles(finish)


def cells(entries, others, state, coord, bt, mp, of):
    members = state.shape[1]
    tiles = state.shape[0] // CT
    return pl.pallas_call(
        cell_kernel,
        out_shape=jax.ShapeDtypeStruct(state.shape, BF16),
        in_specs=[in_smem()] * 2 + [in_vmem()] * 5,
        out_specs=in_vmem(),
        scratch_shapes=[
            pltpu.VMEM((tiles + 1, CT, members), F32),
            pltpu.VMEM((tiles + 1, CT, members), BF16),
            pltpu.VMEM((tiles + 1, CT, 16), BF16),
            pltpu.VMEM((GROUP, CT, 2 * OBS_DEV), BF16),
            pltpu.VMEM((16, tiles * CT), F32),
        ],
        compiler_params=pltpu.CompilerParams(vmem_limit_bytes=VMEM_LIMIT),
        name="cell_updates",
    )(entries, others, state, coord, bt, mp, of)


def local(
    state,
    cell_coordinate,
    member_predictions,
    measured_values,
    obs_error_variance,
    observation_coordinate,
    localization_tile_pairs,
    used_pair_count,
):
    obs_tiles = lax.axis_size("cell")
    batches = lax.axis_size("dp")
    tiles = state.shape[0] // CT
    mine = pack(member_predictions[0], measured_values, obs_error_variance, observation_coordinate[0])

    def meanwhile(near):
        near, pairs, counts = lax.optimization_barrier((near, localization_tile_pairs[0], used_pair_count[0]))
        return near, pair_lists(pairs, counts, tiles, obs_tiles)

    pieces, (entries, others) = gathered(mine, meanwhile)
    bt, mp, of = chain(pieces, obs_tiles, batches)
    return cells(entries, others, state, cell_coordinate, bt, mp, of)


def solution(mesh):
    placed = (
        P(("cell", "dp"), None),
        P(None, ("cell", "dp")),
        P("dp", "cell", None),
        P("dp", "cell"),
        P("dp", "cell"),
        P("dp", None, "cell"),
        P(("cell", "dp"), None, None, None),
        P(("cell", "dp"), None),
    )
    return jax.shard_map(
        local, mesh=mesh, in_specs=placed, out_specs=P(("cell", "dp"), None), check_vma=False
    )
```

```python
import functools
import math

import jax
import jax.numpy as jnp
from jax import lax
from jax.experimental import pallas as pl
from jax.experimental.pallas import tpu as pltpu
from jax.sharding import PartitionSpec as P

CT = 128
OBS_DEV = 128
EXTRA = 16
taper_rate = 2.0
LOG2E = math.log2(math.e)
GROUP = 4
F32 = jnp.float32
BF16 = jnp.bfloat16
VMEM_LIMIT = 56 * 1024 * 1024


def in_vmem():
    return pl.BlockSpec(memory_space=pltpu.VMEM)


def in_smem():
    return pl.BlockSpec(memory_space=pltpu.SMEM)


def parts(x):
    hi = x.astype(BF16)
    rest = x - hi.astype(F32)
    mid = rest.astype(BF16)
    return hi, mid, (rest - mid.astype(F32)).astype(BF16)


def mm16(a, b):
    return jnp.dot(a, b, preferred_element_type=F32)


def mm_parts(a, b):
    left = jnp.concatenate([a[0], a[0], a[1], a[0], a[1], a[2]], axis=1)
    right = jnp.concatenate([b[0], b[1], b[0], b[2], b[1], b[0]], axis=0)
    return mm16(left, right)


def mm(a, b):
    return mm_parts(parts(a), parts(b))


def pack_kernel(pred, value, variance, coord, out):
    members = pred.shape[1]
    out[:members, :] = pred[...].astype(F32).T.astype(BF16)
    place = coord[...].astype(F32)
    lines = parts(value[...]) + parts(variance[...]) + tuple(place[j : j + 1] for j in range(3))
    out[members:, :] = stacked(lines).astype(BF16)


def pack(pred, value, variance, coord):
    return pl.pallas_call(
        pack_kernel,
        out_shape=jax.ShapeDtypeStruct((pred.shape[1] + EXTRA, pred.shape[0]), BF16),
        in_specs=[in_vmem()] * 4,
        out_specs=in_vmem(),
        name="pack_observations",
    )(pred, value, variance, coord)


def steps_of(size):
    return size.bit_length() - 1


def place_of(mask, size):
    steps = steps_of(size)
    return sum(((mask >> (steps - 1 - s)) & 1) << s for s in range(steps))


def swapped(block, axis, mask):
    return lax.ppermute(block, axis, [(i, i ^ mask) for i in range(lax.axis_size(axis))])


def gathered(mine, meanwhile):
    near = mine[None]
    for b in reversed(range(steps_of(lax.axis_size("cell")))):
        near = jnp.concatenate([near, swapped(near, "cell", 1 << b)], axis=0)
    near, work = meanwhile(near)
    pieces = {0: near}
    mask = lax.axis_size("dp") // 2
    while mask:
        for d in list(pieces):
            pieces[d ^ mask] = swapped(pieces[d], "dp", mask)
        if len(pieces) == 2:
            pieces[mask], work = lax.optimization_barrier((pieces[mask], work))
        mask //= 2
    return [pieces[d] for d in range(len(pieces))], work


def inverse_of(eye, s, both):
    n = s.shape[0]
    bound = jnp.max(jnp.sum(jnp.abs(s), axis=0, keepdims=True))
    scale = 2.0 / (2.0 + bound)
    rho = bound / (2.0 + bound)
    both[:n] = eye - scale * (eye + s)

    def advance(rho, square, total):
        by = 1.0 / (2.0 - rho * rho)
        both[:n] = (2.0 * by) * square - (rho * rho * by) * eye
        both[n:] = (2.0 * by) * total
        return rho * rho * by

    r = both[:n]
    rho = advance(rho, mm(r, r), eye + r)

    def more(carry):
        rho, left = carry
        return (rho > 1e-8) & (left > 0)

    def factor(carry):
        rho, left = carry
        old = both[...]
        pieces = parts(old)
        new = mm_parts(pieces, [p[:n] for p in pieces])
        return advance(rho, new[:n], old[n:] + new[n:]), left - 1

    lax.while_loop(more, factor, (rho, jnp.int32(40)))
    return scale * both[n:]


def stacked(lines):
    width = lines[0].shape[1]
    rows = lax.broadcasted_iota(jnp.int32, (16, width), 0)
    out = jnp.zeros((16, width), F32)
    for j, line in enumerate(lines):
        out = jnp.where(rows == j, line.astype(F32), out)
    return out


def norm_parts(place):
    return parts(-taper_rate * LOG2E * jnp.sum(place * place, axis=0, keepdims=True))


def cell_features(place):
    ones = [jnp.ones((1, place.shape[1]), F32)] * 3
    return stacked([place[j : j + 1] for j in range(3)] * 3 + list(norm_parts(place)) + ones)


def obs_features(place):
    ones = [jnp.ones((1, place.shape[1]), F32)] * 3
    scaled = parts(place * (2 * taper_rate * LOG2E))
    lines = [part[j : j + 1].astype(F32) for part in scaled for j in range(3)]
    return stacked(lines + ones + list(norm_parts(place))).astype(BF16)


def chain_kernel(*refs):
    pieces, (bt_out, mp_out, of_out, ys, wd, gs, us, both_ref) = refs[:-8], refs[-8:]
    batches, tiles = bt_out.shape[:2]
    members = bt_out.shape[2]
    rows = lax.broadcasted_iota(jnp.int32, (members, members), 0)
    cols = lax.broadcasted_iota(jnp.int32, (members, members), 1)
    eye = jnp.where(rows == cols, 1.0, 0.0)
    my_tile, my_batch = lax.axis_index("cell"), lax.axis_index("dp")

    for rd in range(batches):
        lefts, rights = [], []
        k = my_batch ^ rd
        for rc in range(tiles):
            u = my_tile ^ rc
            r = place_of(rc, tiles)
            raw = pieces[rd][r, :members, :]
            y = raw.astype(F32)
            e = pieces[rd][r, members:, :].astype(F32)
            value = e[0:1] + e[1:2] + e[2:3]
            variance = e[3:4] + e[4:5] + e[5:6]
            place = e[6:9]
            mean = jnp.mean(y, axis=0, keepdims=True)
            w = 1.0 / variance
            where = pl.ds(pl.multiple_of(u * OBS_DEV, OBS_DEV), OBS_DEV)
            ys[k, :, where] = raw
            wd[k, 0:1, where] = w
            wd[k, 1:2, where] = value
            of_out[k, u] = obs_features(place)
            z = jnp.broadcast_to((value - mean) * w, (16, OBS_DEV))
            lefts.append(jnp.concatenate(parts(jnp.concatenate([(y - mean) * w, z], axis=0)), axis=0))
            rights.append(raw)
        g = lax.dot_general(
            jnp.concatenate(lefts, axis=1), jnp.concatenate(rights, axis=1), (((1,), (1,)), ((), ())),
            preferred_element_type=F32,
        )
        n = members + 16
        g = g[:n] + g[n : 2 * n] + g[2 * n :]
        g = g - jnp.mean(g, axis=1, keepdims=True)
        gs[k] = g[:members]
        us[k] = g[members:]

    qt = eye - 1.0 / members
    p = jnp.full((16, members), 1.0 / members, F32)
    chunk = min(2, tiles) * OBS_DEV
    for k in range(batches):
        inverse = inverse_of(eye, gs[k] * (1.0 / (members - 1)), both_ref)
        inverse_parts = parts(inverse)
        qt_parts = parts(qt)
        mt = mm_parts(inverse_parts, qt_parts)
        ht = 0.5 * qt + p[0:1]
        hi, mid, lo = parts(jnp.concatenate([mt, ht], axis=0))
        twice = jnp.concatenate([hi, mid], axis=1)
        for n in range(tiles * OBS_DEV // chunk):
            where = pl.ds(n * chunk, chunk)
            y = ys[k, :, where]
            both = mm16(twice, jnp.concatenate([y, y], axis=0)) + mm16(lo, y)
            b = (both[:members] * (1.0 / (members - 1))).astype(BF16)
            pull = wd[k, 0:1, where] * (wd[k, 1:2, where] - both[members:])
            for c in range(chunk // OBS_DEV):
                u = n * (chunk // OBS_DEV) + c
                bt_out[k, u] = b[:, c * OBS_DEV : (c + 1) * OBS_DEV]
                mp_out[k, u] = pull[:, c * OBS_DEV : (c + 1) * OBS_DEV].T.astype(BF16)
        if k + 1 < batches:
            half = parts(0.5 * (eye + inverse))
            step = parts(mm_parts(parts(us[k]), inverse_parts) * (1.0 / (members - 1)))
            p = p + mm_parts(step, qt_parts)
            qt = 0.5 * (qt + mt)
            for j in range(k + 1, batches):
                g_j = parts(gs[j])
                gs[j] = mm_parts(half, parts(mm_parts(g_j, half)))
                us[j] = mm_parts(parts(us[j] - mm_parts(step, g_j)), half)


def chain(pieces, tiles, batches):
    members = pieces[0].shape[1] - EXTRA
    return pl.pallas_call(
        chain_kernel,
        out_shape=(
            jax.ShapeDtypeStruct((batches, tiles, members, OBS_DEV), BF16),
            jax.ShapeDtypeStruct((batches, tiles, OBS_DEV, members), BF16),
            jax.ShapeDtypeStruct((batches, tiles, 16, OBS_DEV), BF16),
        ),
        in_specs=[in_vmem()] * len(pieces),
        out_specs=(in_vmem(),) * 3,
        scratch_shapes=[
            pltpu.VMEM((batches, members, tiles * OBS_DEV), BF16),
            pltpu.VMEM((batches, 8, tiles * OBS_DEV), F32),
            pltpu.VMEM((batches, members, members), F32),
            pltpu.VMEM((batches, 16, members), F32),
            pltpu.VMEM((2 * members, members), F32),
        ],
        compiler_params=pltpu.CompilerParams(vmem_limit_bytes=VMEM_LIMIT),
        name="serial_transforms",
    )(*pieces)


def list_kernel(sizes_in, pairs, entries, *, tiles, obs_tiles):
    batches, _, slots = pairs.shape
    length = entries.shape[1]
    line = lax.broadcasted_iota(jnp.int32, (slots, slots), 1)
    down = lax.broadcasted_iota(jnp.int32, (slots, slots), 0)
    slot = lax.broadcasted_iota(jnp.int32, (slots, length), 1)

    def ones(mask, axis):
        return jnp.sum(jnp.where(mask, 1, 0), axis=axis, keepdims=True)

    row_codes = [pairs[k, 1:2, :] * tiles + pairs[k, 0:1, :] for k in range(batches)]
    row_codes = jnp.concatenate(row_codes + [jnp.zeros((8 - batches, slots), jnp.int32)], axis=0)
    col_codes = row_codes.astype(F32).T.astype(jnp.int32)
    for k in range(batches):
        used = sizes_in[k]
        row = row_codes[k : k + 1]
        col = col_codes[:, k : k + 1]
        row = jnp.where(line[:1] < used, row, tiles * obs_tiles)
        col = jnp.where(down[:, :1] < used, col, tiles * obs_tiles)
        row_u, col_u = row // tiles, col // tiles
        same = row == col
        times = ones(same, 1)
        first_row = (ones(same & (down < line), 0) == 0) & (row_u < obs_tiles)
        first_col = (ones(same & (line < down), 1) == 0) & (col_u < obs_tiles)
        mates = row_u == col_u
        lead_row = first_row & (ones(first_col & mates & (col < row), 0) % GROUP == 0)
        within = ones(first_row & mates & (row < col), 1) % GROUP
        place = (ones(lead_row & (row <= col), 1) - 1) * GROUP + within
        value = ((col - col_u * tiles) << 16) + (col_u << 10) + times
        entry = jnp.sum(jnp.where(first_col & (place == slot), value, 0), axis=0, keepdims=True)
        entry = jnp.where(entry > 0, entry, tiles << 16)
        entries[k : k + 1, :] = jnp.where(slot[:1] == length - 1, ones(lead_row, 1), entry)


def pair_lists(pairs, counts, tiles, obs_tiles):
    batches, slots = pairs.shape[0], pairs.shape[2]
    most = slots + (GROUP - 1) * obs_tiles + 1
    return pl.pallas_call(
        functools.partial(list_kernel, tiles=tiles, obs_tiles=obs_tiles),
        out_shape=jax.ShapeDtypeStruct((batches, -(-most // 128) * 128), jnp.int32),
        in_specs=[in_smem(), in_vmem()],
        out_specs=in_vmem(),
        cost_estimate=pl.CostEstimate(flops=40 * batches * slots * slots, bytes_accessed=16 * batches * slots, transcendentals=0),
        name="pair_lists",
    )(counts, pairs)


def cell_kernel(entries, state, coord, bt, mp, of, out, acc, left, right, held, tall):
    batches, obs_tiles = bt.shape[:2]
    members = state.shape[1]
    tiles = state.shape[0] // CT
    several = 4 if tiles % 4 == 0 else 1
    tall[...] = cell_features(coord[...].astype(F32))

    def over_tiles(body):
        def some(i, _):
            for j in range(several):
                body(i * several + j)
            return 0

        lax.fori_loop(0, tiles // several, some, 0)

    def prepare(t):
        where = pl.ds(pl.multiple_of(t * CT, CT), CT)
        acc[t] = state[where, :].astype(F32)
        left[t, :, members:] = jnp.concatenate([tall[:, where].T.astype(BF16), jnp.zeros((CT, members - 16), BF16)], axis=1)

    over_tiles(prepare)
    acc[tiles] = jnp.zeros((CT, members), F32)
    left[tiles] = jnp.zeros((CT, 2 * members), BF16)
    right[...] = jnp.zeros(right.shape, BF16)

    for k in range(batches):

        def centre(t):
            x = acc[t]
            left[t, :, :members] = ((x - jnp.mean(x, axis=1, keepdims=True))).astype(BF16)

        over_tiles(centre)

        for u in range(obs_tiles):
            right[u, :members, :OBS_DEV] = bt[k, u]
            right[u, members : members + 16, OBS_DEV:] = of[k, u]

        def named(i):
            group = [entries[k, i * GROUP + j] for j in range(GROUP)]
            return (group[0] >> 10) & 63, [e >> 16 for e in group], [e & 1023 for e in group]

        def weigh(i):
            u, ts, ms = named(i)
            both = mm16(jnp.concatenate([left[t] for t in ts], axis=0), right[u])
            for j, m in enumerate(ms):
                rows = slice(j * CT, (j + 1) * CT)
                held[rows, :] = (jnp.exp2(both[rows, OBS_DEV:]) * (both[rows, :OBS_DEV] * m.astype(F32))).astype(BF16)

        def pull(i):
            u, ts, _ = named(i)
            terms = mm16(held[...], mp[k, u])
            for j, t in enumerate(ts):
                acc[t] += terms[j * CT : (j + 1) * CT]

        def group(i, _):
            pull(i - 1)
            weigh(i)
            return 0

        groups = entries[k, entries.shape[1] - 1]
        weigh(0)
        lax.fori_loop(1, groups, group, 0)
        pull(groups - 1)

    def finish(t):
        out[pl.ds(pl.multiple_of(t * CT, CT), CT), :] = acc[t].astype(BF16)

    over_tiles(finish)


def cells(entries, state, coord, bt, mp, of):
    members = state.shape[1]
    tiles = state.shape[0] // CT
    return pl.pallas_call(
        cell_kernel,
        out_shape=jax.ShapeDtypeStruct(state.shape, BF16),
        in_specs=[in_smem()] + [in_vmem()] * 5,
        out_specs=in_vmem(),
        scratch_shapes=[
            pltpu.VMEM((tiles + 1, CT, members), F32),
            pltpu.VMEM((tiles + 1, CT, 2 * members), BF16),
            pltpu.VMEM((bt.shape[1], 2 * members, 2 * OBS_DEV), BF16),
            pltpu.VMEM((GROUP * CT, OBS_DEV), BF16),
            pltpu.VMEM((16, tiles * CT), F32),
        ],
        compiler_params=pltpu.CompilerParams(vmem_limit_bytes=VMEM_LIMIT),
        name="cell_updates",
    )(entries, state, coord, bt, mp, of)


def local(
    state,
    cell_coordinate,
    member_predictions,
    measured_values,
    obs_error_variance,
    observation_coordinate,
    localization_tile_pairs,
    used_pair_count,
):
    obs_tiles = lax.axis_size("cell")
    batches = lax.axis_size("dp")
    tiles = state.shape[0] // CT
    mine = pack(member_predictions[0], measured_values, obs_error_variance, observation_coordinate[0])

    def meanwhile(near):
        near, pairs, counts = lax.optimization_barrier((near, localization_tile_pairs[0], used_pair_count[0]))
        return near, pair_lists(pairs, counts, tiles, obs_tiles)

    pieces, entries = gathered(mine, meanwhile)
    bt, mp, of = chain(pieces, obs_tiles, batches)
    return cells(entries, state, cell_coordinate, bt, mp, of)


def solution(mesh):
    placed = (
        P(("cell", "dp"), None),
        P(None, ("cell", "dp")),
        P("dp", "cell", None),
        P("dp", "cell"),
        P("dp", "cell"),
        P("dp", None, "cell"),
        P(("cell", "dp"), None, None, None),
        P(("cell", "dp"), None),
    )
    return jax.shard_map(
        local, mesh=mesh, in_specs=placed, out_specs=P(("cell", "dp"), None), check_vma=False
    )
```

```python
import functools
import math

import jax
import jax.numpy as jnp
from jax import lax
from jax.experimental import pallas as pl
from jax.experimental.pallas import tpu as pltpu
from jax.sharding import PartitionSpec as P

CT = 128
OBS_DEV = 128
EXTRA = 16
taper_rate = 2.0
LOG2E = math.log2(math.e)
GROUP = 8
F32 = jnp.float32
BF16 = jnp.bfloat16
VMEM_LIMIT = 56 * 1024 * 1024


def in_vmem():
    return pl.BlockSpec(memory_space=pltpu.VMEM)


def in_smem():
    return pl.BlockSpec(memory_space=pltpu.SMEM)


def parts(x):
    hi = x.astype(BF16)
    rest = x - hi.astype(F32)
    mid = rest.astype(BF16)
    return hi, mid, (rest - mid.astype(F32)).astype(BF16)


def mm16(a, b):
    return jnp.dot(a, b, preferred_element_type=F32)


def mm_parts(a, b):
    left = jnp.concatenate([a[0], a[0], a[1], a[0], a[1], a[2]], axis=1)
    right = jnp.concatenate([b[0], b[1], b[0], b[2], b[1], b[0]], axis=0)
    return mm16(left, right)


def mm(a, b):
    return mm_parts(parts(a), parts(b))


def pack_kernel(pred, value, variance, coord, out):
    members = pred.shape[1]
    out[:members, :] = pred[...].astype(F32).T.astype(BF16)
    place = coord[...].astype(F32)
    lines = parts(value[...]) + parts(variance[...]) + tuple(place[j : j + 1] for j in range(3))
    out[members:, :] = stacked(lines).astype(BF16)


def pack(pred, value, variance, coord):
    return pl.pallas_call(
        pack_kernel,
        out_shape=jax.ShapeDtypeStruct((pred.shape[1] + EXTRA, pred.shape[0]), BF16),
        in_specs=[in_vmem()] * 4,
        out_specs=in_vmem(),
        name="pack_observations",
    )(pred, value, variance, coord)


def steps_of(size):
    return size.bit_length() - 1


def place_of(mask, size):
    steps = steps_of(size)
    return sum(((mask >> (steps - 1 - s)) & 1) << s for s in range(steps))


def swapped(block, axis, mask):
    return lax.ppermute(block, axis, [(i, i ^ mask) for i in range(lax.axis_size(axis))])


def gathered(mine, meanwhile):
    near = mine[None]
    for b in reversed(range(steps_of(lax.axis_size("cell")))):
        near = jnp.concatenate([near, swapped(near, "cell", 1 << b)], axis=0)
    near, work = meanwhile(near)
    pieces = {0: near}
    mask = lax.axis_size("dp") // 2
    while mask:
        for d in list(pieces):
            pieces[d ^ mask] = swapped(pieces[d], "dp", mask)
        if len(pieces) == 2:
            pieces[mask], work = lax.optimization_barrier((pieces[mask], work))
        mask //= 2
    return [pieces[d] for d in range(len(pieces))], work


def inverse_of(eye, s, both):
    n = s.shape[0]
    bound = jnp.max(jnp.sum(jnp.abs(s), axis=0, keepdims=True))
    scale = 2.0 / (2.0 + bound)
    rho = bound / (2.0 + bound)
    both[:n] = eye - scale * (eye + s)

    def advance(rho, square, total):
        by = 1.0 / (2.0 - rho * rho)
        both[:n] = (2.0 * by) * square - (rho * rho * by) * eye
        both[n:] = (2.0 * by) * total
        return rho * rho * by

    r = both[:n]
    rho = advance(rho, mm(r, r), eye + r)

    def more(carry):
        rho, left = carry
        return (rho > 1e-8) & (left > 0)

    def factor(carry):
        rho, left = carry
        old = both[...]
        pieces = parts(old)
        new = mm_parts(pieces, [p[:n] for p in pieces])
        return advance(rho, new[:n], old[n:] + new[n:]), left - 1

    lax.while_loop(more, factor, (rho, jnp.int32(40)))
    return scale * both[n:]


def stacked(lines):
    width = lines[0].shape[1]
    rows = lax.broadcasted_iota(jnp.int32, (16, width), 0)
    out = jnp.zeros((16, width), F32)
    for j, line in enumerate(lines):
        out = jnp.where(rows == j, line.astype(F32), out)
    return out


def chain_kernel(*refs):
    pieces, (bt_out, mp_out, oc_out, ys, wd, gs, us, both_ref) = refs[:-8], refs[-8:]
    batches, tiles = bt_out.shape[:2]
    members = bt_out.shape[2]
    rows = lax.broadcasted_iota(jnp.int32, (members, members), 0)
    cols = lax.broadcasted_iota(jnp.int32, (members, members), 1)
    eye = jnp.where(rows == cols, 1.0, 0.0)
    my_tile, my_batch = lax.axis_index("cell"), lax.axis_index("dp")

    for rd in range(batches):
        lefts, rights = [], []
        k = my_batch ^ rd
        for rc in range(tiles):
            u = my_tile ^ rc
            r = place_of(rc, tiles)
            raw = pieces[rd][r, :members, :]
            y = raw.astype(F32)
            e = pieces[rd][r, members:, :].astype(F32)
            value = e[0:1] + e[1:2] + e[2:3]
            variance = e[3:4] + e[4:5] + e[5:6]
            place = e[6:9]
            mean = jnp.mean(y, axis=0, keepdims=True)
            w = 1.0 / variance
            where = pl.ds(pl.multiple_of(u * OBS_DEV, OBS_DEV), OBS_DEV)
            ys[k, :, where] = raw
            wd[k, 0:1, where] = w
            wd[k, 1:2, where] = value
            wd[k, 2:3, where] = jnp.exp(-taper_rate * jnp.sum(place * place, axis=0, keepdims=True)) * (1.0 / (members - 1))
            oc_out[k, u] = jnp.concatenate([place * (2 * taper_rate * LOG2E), jnp.zeros((5, OBS_DEV), F32)], axis=0)
            z = jnp.broadcast_to((value - mean) * w, (16, OBS_DEV))
            lefts.append(jnp.concatenate(parts(jnp.concatenate([(y - mean) * w, z], axis=0)), axis=0))
            rights.append(raw)
        g = lax.dot_general(
            jnp.concatenate(lefts, axis=1), jnp.concatenate(rights, axis=1), (((1,), (1,)), ((), ())),
            preferred_element_type=F32,
        )
        n = members + 16
        g = g[:n] + g[n : 2 * n] + g[2 * n :]
        g = g - jnp.mean(g, axis=1, keepdims=True)
        gs[k] = g[:members]
        us[k] = g[members:]

    qt = eye - 1.0 / members
    p = jnp.full((16, members), 1.0 / members, F32)
    chunk = min(2, tiles) * OBS_DEV
    for k in range(batches):
        inverse = inverse_of(eye, gs[k] * (1.0 / (members - 1)), both_ref)
        inverse_parts = parts(inverse)
        qt_parts = parts(qt)
        mt = mm_parts(inverse_parts, qt_parts)
        ht = 0.5 * qt + p[0:1]
        hi, mid, lo = parts(jnp.concatenate([mt, ht], axis=0))
        twice = jnp.concatenate([hi, mid], axis=1)
        for n in range(tiles * OBS_DEV // chunk):
            where = pl.ds(n * chunk, chunk)
            y = ys[k, :, where]
            both = mm16(twice, jnp.concatenate([y, y], axis=0)) + mm16(lo, y)
            b = (both[:members] * wd[k, 2:3, where]).astype(BF16)
            pull = wd[k, 0:1, where] * (wd[k, 1:2, where] - both[members:])
            for c in range(chunk // OBS_DEV):
                u = n * (chunk // OBS_DEV) + c
                bt_out[k, u] = b[:, c * OBS_DEV : (c + 1) * OBS_DEV]
                mp_out[k, u] = pull[:, c * OBS_DEV : (c + 1) * OBS_DEV].T.astype(BF16)
        if k + 1 < batches:
            half = parts(0.5 * (eye + inverse))
            step = parts(mm_parts(parts(us[k]), inverse_parts) * (1.0 / (members - 1)))
            p = p + mm_parts(step, qt_parts)
            qt = 0.5 * (qt + mt)
            for j in range(k + 1, batches):
                g_j = parts(gs[j])
                gs[j] = mm_parts(half, parts(mm_parts(g_j, half)))
                us[j] = mm_parts(parts(us[j] - mm_parts(step, g_j)), half)


def chain(pieces, tiles, batches):
    members = pieces[0].shape[1] - EXTRA
    return pl.pallas_call(
        chain_kernel,
        out_shape=(
            jax.ShapeDtypeStruct((batches, tiles, members, OBS_DEV), BF16),
            jax.ShapeDtypeStruct((batches, tiles, OBS_DEV, members), BF16),
            jax.ShapeDtypeStruct((batches, tiles, 8, OBS_DEV), F32),
        ),
        in_specs=[in_vmem()] * len(pieces),
        out_specs=(in_vmem(),) * 3,
        scratch_shapes=[
            pltpu.VMEM((batches, members, tiles * OBS_DEV), BF16),
            pltpu.VMEM((batches, 8, tiles * OBS_DEV), F32),
            pltpu.VMEM((batches, members, members), F32),
            pltpu.VMEM((batches, 16, members), F32),
            pltpu.VMEM((2 * members, members), F32),
        ],
        compiler_params=pltpu.CompilerParams(vmem_limit_bytes=VMEM_LIMIT),
        name="serial_transforms",
    )(*pieces)


def list_kernel(sizes_in, pairs, entries, others, *, tiles, obs_tiles):
    batches, _, slots = pairs.shape
    length = entries.shape[1]
    line = lax.broadcasted_iota(jnp.int32, (slots, slots), 1)
    down = lax.broadcasted_iota(jnp.int32, (slots, slots), 0)
    slot = lax.broadcasted_iota(jnp.int32, (slots, length), 1)

    def ones(mask, axis):
        return jnp.sum(jnp.where(mask, 1, 0), axis=axis, keepdims=True)

    row_codes = [pairs[k, 0:1, :] * obs_tiles + pairs[k, 1:2, :] for k in range(batches)]
    row_codes = jnp.concatenate(row_codes + [jnp.zeros((8 - batches, slots), jnp.int32)], axis=0)
    col_codes = row_codes.astype(F32).T.astype(jnp.int32)
    for k in range(batches):
        used = sizes_in[k]
        row = row_codes[k : k + 1]
        col = col_codes[:, k : k + 1]
        row = jnp.where(line[:1] < used, row, tiles * obs_tiles)
        col = jnp.where(down[:, :1] < used, col, tiles * obs_tiles)
        row_t, col_t = row // obs_tiles, col // obs_tiles
        same = row == col
        times = ones(same, 1)
        first_row = (ones(same & (down < line), 0) == 0) & (row_t < tiles)
        first_col = (ones(same & (line < down), 1) == 0) & (col_t < tiles)
        mates = row_t == col_t
        even_row = (ones(first_col & mates & (col < row), 0) & 1) == 0
        even_col = (ones(first_row & mates & (row < col), 1) & 1) == 0
        place = ones(first_row & even_row & (row <= col), 1) - 1
        here = first_col & (place == slot)
        value = ((col - col_t * obs_tiles) << 10) + times
        size = ones(first_row & even_row, 1)
        entry = jnp.sum(jnp.where(here & even_col, value + (col_t << 16), 0), axis=0, keepdims=True)
        other = jnp.sum(jnp.where(here & ~even_col, value, 0), axis=0, keepdims=True)
        entries[k : k + 1, :] = jnp.where(entry > 0, entry, tiles << 16)
        others[k : k + 1, :] = jnp.where(slot[:1] == length - 1, size, other)


def pair_lists(pairs, counts, tiles, obs_tiles):
    batches, slots = pairs.shape[0], pairs.shape[2]
    shape = jax.ShapeDtypeStruct((batches, -(-(slots + GROUP) // 128) * 128), jnp.int32)
    return pl.pallas_call(
        functools.partial(list_kernel, tiles=tiles, obs_tiles=obs_tiles),
        out_shape=(shape, shape),
        in_specs=[in_smem(), in_vmem()],
        out_specs=(in_vmem(),) * 2,
        cost_estimate=pl.CostEstimate(flops=40 * batches * slots * slots, bytes_accessed=16 * batches * slots, transcendentals=0),
        name="pair_lists",
    )(counts, pairs)


def cell_kernel(entries, others, state, coord, bt, mp, oc, out, acc, pert, cb, ec, held, tall):
    batches, obs_tiles = bt.shape[:2]
    members = state.shape[1]
    tiles = state.shape[0] // CT
    several = 4 if tiles % 4 == 0 else 1
    tall[:3, :] = coord[...].astype(F32)

    def over_tiles(body):
        def some(i, _):
            for j in range(several):
                body(i * several + j)
            return 0

        lax.fori_loop(0, tiles // several, some, 0)

    def prepare(t):
        where = pl.ds(pl.multiple_of(t * CT, CT), CT)
        acc[t] = state[where, :].astype(F32)
        place = tall[:, where].T
        norm = jnp.zeros((CT, members), F32)
        for j in range(3):
            c = jnp.broadcast_to(place[:, j : j + 1], (CT, members))
            cb[j, t] = c
            norm = norm + c * c
        ec[t] = jnp.exp(-taper_rate * norm)

    over_tiles(prepare)
    acc[tiles] = jnp.zeros((CT, members), F32)
    pert[tiles] = jnp.zeros((CT, members), BF16)
    for j in range(3):
        cb[j, tiles] = jnp.zeros((CT, members), F32)

    for k in range(batches):

        def centre(t):
            x = acc[t]
            pert[t] = ((x - jnp.mean(x, axis=1, keepdims=True)) * ec[t]).astype(BF16)

        over_tiles(centre)

        def named(i, j):
            e, o = entries[k, i * GROUP + j], others[k, i * GROUP + j]
            return e >> 16, (e >> 10) & 63, o >> 10, e & 1023, o & 1023

        def weigh(i):
            for j in range(GROUP):
                t, u0, u1, m0, m1 = named(i, j)
                score = mm16(pert[t], jnp.concatenate([bt[k, u0], bt[k, u1]], axis=1))
                sides = [(oc[k, u], m.astype(F32)) for u, m in ((u0, m0), (u1, m1))]
                for r in range(0, CT, 16):
                    c = [cb[axis, t, r : r + 16, :] for axis in range(3)]
                    for n, (o, m) in enumerate(sides):
                        cut = slice(n * OBS_DEV, (n + 1) * OBS_DEV)
                        x = c[0] * o[0:1] + c[1] * o[1:2] + c[2] * o[2:3]
                        held[j, r : r + 16, cut] = (jnp.exp2(x) * (score[r : r + 16, cut] * m)).astype(BF16)

        def pull(i):
            for j in range(GROUP):
                t, u0, u1, _, _ = named(i, j)
                acc[t] += mm16(held[j], jnp.concatenate([mp[k, u0], mp[k, u1]], axis=0))

        def group(i, _):
            pull(i - 1)
            weigh(i)
            return 0

        groups = (others[k, others.shape[1] - 1] + GROUP - 1) // GROUP
        weigh(0)
        lax.fori_loop(1, groups, group, 0)
        pull(groups - 1)

    def finish(t):
        out[pl.ds(pl.multiple_of(t * CT, CT), CT), :] = acc[t].astype(BF16)

    over_tiles(finish)


def cells(entries, others, state, coord, bt, mp, oc):
    members = state.shape[1]
    tiles = state.shape[0] // CT
    return pl.pallas_call(
        cell_kernel,
        out_shape=jax.ShapeDtypeStruct(state.shape, BF16),
        in_specs=[in_smem()] * 2 + [in_vmem()] * 5,
        out_specs=in_vmem(),
        scratch_shapes=[
            pltpu.VMEM((tiles + 1, CT, members), F32),
            pltpu.VMEM((tiles + 1, CT, members), BF16),
            pltpu.VMEM((3, tiles + 1, CT, members), F32),
            pltpu.VMEM((tiles, CT, members), F32),
            pltpu.VMEM((GROUP, CT, 2 * OBS_DEV), BF16),
            pltpu.VMEM((8, tiles * CT), F32),
        ],
        compiler_params=pltpu.CompilerParams(vmem_limit_bytes=VMEM_LIMIT),
        name="cell_updates",
    )(entries, others, state, coord, bt, mp, oc)


def local(
    state,
    cell_coordinate,
    member_predictions,
    measured_values,
    obs_error_variance,
    observation_coordinate,
    localization_tile_pairs,
    used_pair_count,
):
    obs_tiles = lax.axis_size("cell")
    batches = lax.axis_size("dp")
    tiles = state.shape[0] // CT
    mine = pack(member_predictions[0], measured_values, obs_error_variance, observation_coordinate[0])

    def meanwhile(near):
        near, pairs, counts = lax.optimization_barrier((near, localization_tile_pairs[0], used_pair_count[0]))
        return near, pair_lists(pairs, counts, tiles, obs_tiles)

    pieces, (entries, others) = gathered(mine, meanwhile)
    bt, mp, oc = chain(pieces, obs_tiles, batches)
    return cells(entries, others, state, cell_coordinate, bt, mp, oc)


def solution(mesh):
    placed = (
        P(("cell", "dp"), None),
        P(None, ("cell", "dp")),
        P("dp", "cell", None),
        P("dp", "cell"),
        P("dp", "cell"),
        P("dp", None, "cell"),
        P(("cell", "dp"), None, None, None),
        P(("cell", "dp"), None),
    )
    return jax.shard_map(
        local, mesh=mesh, in_specs=placed, out_specs=P(("cell", "dp"), None), check_vma=False
    )
```

```python
import functools
import math

import jax
import jax.numpy as jnp
from jax import lax
from jax.experimental import pallas as pl
from jax.experimental.pallas import tpu as pltpu
from jax.sharding import PartitionSpec as P

CT = 128
OBS_DEV = 128
EXTRA = 16
taper_rate = 2.0
LOG2E = math.log2(math.e)
GROUP = 8
F32 = jnp.float32
BF16 = jnp.bfloat16
VMEM_LIMIT = 40 * 1024 * 1024


def in_vmem():
    return pl.BlockSpec(memory_space=pltpu.VMEM)


def in_smem():
    return pl.BlockSpec(memory_space=pltpu.SMEM)


def parts(x):
    hi = x.astype(BF16)
    rest = x - hi.astype(F32)
    mid = rest.astype(BF16)
    return hi, mid, (rest - mid.astype(F32)).astype(BF16)


def mm16(a, b):
    return jnp.dot(a, b, preferred_element_type=F32)


def mm_parts(a, b):
    def two(i, j, m, n):
        return mm16(jnp.concatenate([a[i], a[m]], axis=1), jnp.concatenate([b[j], b[n]], axis=0))

    return two(0, 0, 0, 1) + (two(1, 0, 0, 2) + two(1, 1, 2, 0))


def mm(a, b):
    return mm_parts(parts(a), parts(b))


def pack_kernel(pred, value, variance, coord, out):
    members = pred.shape[1]
    out[:members, :] = pred[...].astype(F32).T.astype(BF16)
    place = coord[...].astype(F32)
    lines = parts(value[...]) + parts(variance[...]) + tuple(place[j : j + 1] for j in range(3))
    out[members:, :] = stacked(lines).astype(BF16)


def pack(pred, value, variance, coord):
    return pl.pallas_call(
        pack_kernel,
        out_shape=jax.ShapeDtypeStruct((pred.shape[1] + EXTRA, pred.shape[0]), BF16),
        in_specs=[in_vmem()] * 4,
        out_specs=in_vmem(),
        name="pack_observations",
    )(pred, value, variance, coord)


def steps_of(size):
    return size.bit_length() - 1


def place_of(mask, size):
    steps = steps_of(size)
    return sum(((mask >> (steps - 1 - s)) & 1) << s for s in range(steps))


def swapped(block, axis, mask):
    return lax.ppermute(block, axis, [(i, i ^ mask) for i in range(lax.axis_size(axis))])


def gathered(mine, meanwhile):
    near = mine[None]
    for b in reversed(range(steps_of(lax.axis_size("cell")))):
        near = jnp.concatenate([near, swapped(near, "cell", 1 << b)], axis=0)
    near, work = meanwhile(near)
    pieces = {0: near}
    mask = lax.axis_size("dp") // 2
    while mask:
        for d in list(pieces):
            pieces[d ^ mask] = swapped(pieces[d], "dp", mask)
        if len(pieces) == 2:
            pieces[mask], work = lax.optimization_barrier((pieces[mask], work))
        mask //= 2
    return [pieces[d] for d in range(len(pieces))], work


def inverse_of(eye, s, both):
    n = s.shape[0]
    bound = jnp.max(jnp.sum(jnp.abs(s), axis=0, keepdims=True))
    scale = 2.0 / (2.0 + bound)
    rho = bound / (2.0 + bound)
    both[:n] = eye - scale * (eye + s)

    def advance(rho, square, total):
        by = 1.0 / (2.0 - rho * rho)
        both[:n] = (2.0 * by) * square - (rho * rho * by) * eye
        both[n:] = (2.0 * by) * total
        return rho * rho * by

    r = both[:n]
    rho = advance(rho, mm(r, r), eye + r)

    def more(carry):
        rho, left = carry
        return (rho > 1e-8) & (left > 0)

    def factor(carry):
        rho, left = carry
        old = both[...]
        pieces = parts(old)
        new = mm_parts(pieces, [p[:n] for p in pieces])
        return advance(rho, new[:n], old[n:] + new[n:]), left - 1

    lax.while_loop(more, factor, (rho, jnp.int32(40)))
    return scale * both[n:]


def stacked(lines):
    width = lines[0].shape[1]
    rows = lax.broadcasted_iota(jnp.int32, (16, width), 0)
    out = jnp.zeros((16, width), F32)
    for j, line in enumerate(lines):
        out = jnp.where(rows == j, line.astype(F32), out)
    return out


def norm_parts(place):
    return parts(-taper_rate * LOG2E * jnp.sum(place * place, axis=0, keepdims=True))


def cell_features(place):
    ones = [jnp.ones((1, place.shape[1]), F32)] * 3
    return stacked([place[j : j + 1] for j in range(3)] * 3 + list(norm_parts(place)) + ones)


def obs_features(place):
    ones = [jnp.ones((1, place.shape[1]), F32)] * 3
    scaled = parts(place * (2 * taper_rate * LOG2E))
    lines = [part[j : j + 1].astype(F32) for part in scaled for j in range(3)]
    return stacked(lines + ones + list(norm_parts(place))).astype(BF16)


def list_kernel(sizes_in, pairs, entries, others, *, tiles, obs_tiles):
    batches, _, slots = pairs.shape
    length = entries.shape[1]
    line = lax.broadcasted_iota(jnp.int32, (slots, slots), 1)
    down = lax.broadcasted_iota(jnp.int32, (slots, slots), 0)
    slot = lax.broadcasted_iota(jnp.int32, (slots, length), 1)

    def ones(mask, axis):
        return jnp.sum(jnp.where(mask, 1, 0), axis=axis, keepdims=True)

    row_codes = [pairs[k, 0:1, :] * obs_tiles + pairs[k, 1:2, :] for k in range(batches)]
    row_codes = jnp.concatenate(row_codes + [jnp.zeros((8 - batches, slots), jnp.int32)], axis=0)
    col_codes = row_codes.astype(F32).T.astype(jnp.int32)
    for k in range(batches):
        used = sizes_in[k]
        row = row_codes[k : k + 1]
        col = col_codes[:, k : k + 1]
        row = jnp.where(line[:1] < used, row, tiles * obs_tiles)
        col = jnp.where(down[:, :1] < used, col, tiles * obs_tiles)
        row_t, col_t = row // obs_tiles, col // obs_tiles
        same = row == col
        times = ones(same, 1)
        first_row = (ones(same & (down < line), 0) == 0) & (row_t < tiles)
        first_col = (ones(same & (line < down), 1) == 0) & (col_t < tiles)
        mates = row_t == col_t
        even_row = (ones(first_col & mates & (col < row), 0) & 1) == 0
        even_col = (ones(first_row & mates & (row < col), 1) & 1) == 0
        place = ones(first_row & even_row & (row <= col), 1) - 1
        here = first_col & (place == slot)
        value = ((col - col_t * obs_tiles) << 10) + times
        size = ones(first_row & even_row, 1)
        entry = jnp.sum(jnp.where(here & even_col, value + (col_t << 16), 0), axis=0, keepdims=True)
        other = jnp.sum(jnp.where(here & ~even_col, value, 0), axis=0, keepdims=True)
        entries[k : k + 1, :] = jnp.where(entry > 0, entry, tiles << 16)
        others[k : k + 1, :] = jnp.where(slot[:1] == length - 1, size, other)


def pair_lists(pairs, counts, tiles, obs_tiles):
    batches, slots = pairs.shape[0], pairs.shape[2]
    shape = jax.ShapeDtypeStruct((batches, -(-(slots + GROUP) // 128) * 128), jnp.int32)
    return pl.pallas_call(
        functools.partial(list_kernel, tiles=tiles, obs_tiles=obs_tiles),
        out_shape=(shape, shape),
        in_specs=[in_smem(), in_vmem()],
        out_specs=(in_vmem(),) * 2,
        cost_estimate=pl.CostEstimate(flops=40 * batches * slots * slots, bytes_accessed=16 * batches * slots, transcendentals=0),
        name="pair_lists",
    )(counts, pairs)


def filter_kernel(entries, others, coord, state, *refs, pieces_count):
    pieces, out, scratch = refs[:pieces_count], refs[pieces_count], refs[pieces_count + 1 :]
    blocks, ys, wd, of, gs, us, both_ref, bt, mp, prior, acc, pert, feat, held, tall, final, arrived, left = scratch
    batches, obs_tiles = of.shape[:2]
    members = state.shape[1]
    tiles = state.shape[0] // CT
    several = 4 if tiles % 4 == 0 else 1

    copies = [pltpu.make_async_copy(piece, blocks.at[d], arrived.at[d]) for d, piece in enumerate(pieces)]
    copies.append(pltpu.make_async_copy(state, prior, arrived.at[pieces_count]))
    for copy in copies:
        copy.start()

    rows = lax.broadcasted_iota(jnp.int32, (members, members), 0)
    cols = lax.broadcasted_iota(jnp.int32, (members, members), 1)
    eye = jnp.where(rows == cols, 1.0, 0.0)
    my_tile, my_batch = lax.axis_index("cell"), lax.axis_index("dp")

    tall[...] = cell_features(coord[...].astype(F32))
    acc[tiles] = jnp.zeros((CT, 2 * members), F32)
    pert[tiles] = jnp.zeros((CT, members), BF16)
    feat[tiles] = jnp.zeros((CT, 16), BF16)

    def over_tiles(body):
        def some(i, _):
            for j in range(several):
                body(i * several + j)
            return 0

        lax.fori_loop(0, tiles // several, some, 0)

    def describe(t):
        feat[t] = tall[:, pl.ds(pl.multiple_of(t * CT, CT), CT)].T.astype(BF16)

    over_tiles(describe)

    for rd in range(batches):
        copies[rd].wait()
        lefts, rights = [], []
        k = my_batch ^ rd
        for rc in range(obs_tiles):
            u = my_tile ^ rc
            r = place_of(rc, obs_tiles)
            raw = blocks[rd, r, :members, :]
            y = raw.astype(F32)
            e = blocks[rd, r, members:, :].astype(F32)
            value = e[0:1] + e[1:2] + e[2:3]
            variance = e[3:4] + e[4:5] + e[5:6]
            mean = jnp.mean(y, axis=0, keepdims=True)
            w = 1.0 / variance
            where = pl.ds(pl.multiple_of(u * OBS_DEV, OBS_DEV), OBS_DEV)
            ys[k, :, where] = raw
            wd[k, 0:1, where] = w
            wd[k, 1:2, where] = value
            of[k, u] = obs_features(e[6:9])
            z = jnp.broadcast_to((value - mean) * w, (16, OBS_DEV))
            lefts.append(parts(jnp.concatenate([(y - mean) * w, z], axis=0)))
            rights.append(raw)
        right = jnp.concatenate(rights, axis=1)
        g = sum(
            lax.dot_general(
                jnp.concatenate(part, axis=1), right, (((1,), (1,)), ((), ())), preferred_element_type=F32
            )
            for part in zip(*lefts)
        )
        g = g - jnp.mean(g, axis=1, keepdims=True)
        gs[k] = g[:members]
        us[k] = g[members:]

    copies[pieces_count].wait()

    def prepare(t):
        x = prior[pl.ds(pl.multiple_of(t * CT, CT), CT), :].astype(F32)
        acc[t, :, :members] = x
        acc[t, :, members:] = x - jnp.mean(x, axis=1, keepdims=True)

    over_tiles(prepare)

    qt = eye - 1.0 / members
    p = jnp.full((16, members), 1.0 / members, F32)
    chunk = min(2, obs_tiles) * OBS_DEV
    for k in range(batches):
        inverse = inverse_of(eye, gs[k] * (1.0 / (members - 1)), both_ref)
        inverse_parts = parts(inverse)
        qt_parts = parts(qt)
        mt = mm_parts(inverse_parts, qt_parts)
        ht = 0.5 * qt + p[0:1]
        hi, mid, lo = parts(jnp.concatenate([mt, ht], axis=0))
        twice = jnp.concatenate([hi, mid], axis=1)
        for n in range(obs_tiles * OBS_DEV // chunk):
            where = pl.ds(n * chunk, chunk)
            y = ys[k, :, where]
            both = mm16(twice, jnp.concatenate([y, y], axis=0)) + mm16(lo, y)
            b = (both[:members] * (1.0 / (members - 1))).astype(BF16)
            pull = wd[k, 0:1, where] * (wd[k, 1:2, where] - both[members:])
            pulls = jnp.concatenate([pull, pull - jnp.mean(pull, axis=0, keepdims=True)], axis=0).astype(BF16)
            for c in range(chunk // OBS_DEV):
                u = n * (chunk // OBS_DEV) + c
                bt[u] = b[:, c * OBS_DEV : (c + 1) * OBS_DEV]
                mp[u] = pulls[:, c * OBS_DEV : (c + 1) * OBS_DEV].T
        if k + 1 < batches:
            half = parts(0.5 * (eye + inverse))
            step = parts(mm_parts(parts(us[k]), inverse_parts) * (1.0 / (members - 1)))
            p = p + mm_parts(step, qt_parts)
            qt = 0.5 * (qt + mt)
            for j in range(k + 1, batches):
                g_j = parts(gs[j])
                gs[j] = mm_parts(half, parts(mm_parts(g_j, half)))
                us[j] = mm_parts(parts(us[j] - mm_parts(step, g_j)), half)

        def centre(t):
            pert[t] = acc[t, :, members:].astype(BF16)

        over_tiles(centre)

        def named(i, j):
            e, o = entries[k, i * GROUP + j], others[k, i * GROUP + j]
            return e >> 16, (e >> 10) & 63, o >> 10, e & 1023, o & 1023

        def weigh(i):
            for j in range(GROUP):
                t, u0, u1, m0, m1 = named(i, j)
                score = mm16(pert[t], jnp.concatenate([bt[u0], bt[u1]], axis=1))
                power = mm16(feat[t], jnp.concatenate([of[k, u0], of[k, u1]], axis=1))
                taper = jnp.exp2(power)
                for n, m in enumerate((m0, m1)):
                    cut = slice(n * OBS_DEV, (n + 1) * OBS_DEV)
                    held[j, :, cut] = (taper[:, cut] * (score[:, cut] * m.astype(F32))).astype(BF16)

        def draw(i):
            for j in range(GROUP):
                t, u0, u1, _, _ = named(i, j)
                acc[t] += mm16(held[j], jnp.concatenate([mp[u0], mp[u1]], axis=0))

        def group(i, _):
            draw(i - 1)
            weigh(i)
            return 0

        groups = (others[k, others.shape[1] - 1] + GROUP - 1) // GROUP
        weigh(0)
        lax.fori_loop(1, groups, group, 0)
        draw(groups - 1)

    leaving = []
    for n in range(left.shape[0]):
        share = tiles // left.shape[0]

        def finish(i, _):
            t = n * share + i
            final[pl.ds(pl.multiple_of(t * CT, CT), CT), :] = acc[t, :, :members].astype(BF16)
            return 0

        lax.fori_loop(0, share, finish, 0)
        where = pl.ds(n * share * CT, share * CT)
        leaving.append(pltpu.make_async_copy(final.at[where], out.at[where], left.at[n]))
        leaving[-1].start()
    for copy in leaving:
        copy.wait()


def filtered(entries, others, coord, state, pieces):
    batches = len(pieces)
    obs_tiles, rows = pieces[0].shape[:2]
    members = state.shape[1]
    tiles = state.shape[0] // CT
    shares = 4 if tiles % 4 == 0 else 1
    anywhere = pl.BlockSpec(memory_space=pl.ANY)
    return pl.pallas_call(
        functools.partial(filter_kernel, pieces_count=batches),
        out_shape=jax.ShapeDtypeStruct(state.shape, BF16),
        in_specs=[in_smem()] * 2 + [in_vmem()] + [anywhere] * (1 + batches),
        out_specs=anywhere,
        scratch_shapes=[
            pltpu.VMEM((batches, obs_tiles, rows, OBS_DEV), BF16),
            pltpu.VMEM((batches, members, obs_tiles * OBS_DEV), BF16),
            pltpu.VMEM((batches, 8, obs_tiles * OBS_DEV), F32),
            pltpu.VMEM((batches, obs_tiles, 16, OBS_DEV), BF16),
            pltpu.VMEM((batches, members, members), F32),
            pltpu.VMEM((batches, 16, members), F32),
            pltpu.VMEM((2 * members, members), F32),
            pltpu.VMEM((obs_tiles, members, OBS_DEV), BF16),
            pltpu.VMEM((obs_tiles, OBS_DEV, 2 * members), BF16),
            pltpu.VMEM(state.shape, BF16),
            pltpu.VMEM((tiles + 1, CT, 2 * members), F32),
            pltpu.VMEM((tiles + 1, CT, members), BF16),
            pltpu.VMEM((tiles + 1, CT, 16), BF16),
            pltpu.VMEM((GROUP, CT, 2 * OBS_DEV), BF16),
            pltpu.VMEM((16, tiles * CT), F32),
            pltpu.VMEM(state.shape, BF16),
            pltpu.SemaphoreType.DMA((batches + 1,)),
            pltpu.SemaphoreType.DMA((shares,)),
        ],
        compiler_params=pltpu.CompilerParams(vmem_limit_bytes=VMEM_LIMIT),
        name="filter",
    )(entries, others, coord, state, *pieces)


def local(
    state,
    cell_coordinate,
    member_predictions,
    measured_values,
    obs_error_variance,
    observation_coordinate,
    localization_tile_pairs,
    used_pair_count,
):
    obs_tiles = lax.axis_size("cell")
    batches = lax.axis_size("dp")
    tiles = state.shape[0] // CT
    mine = pack(member_predictions[0], measured_values, obs_error_variance, observation_coordinate[0])

    def meanwhile(near):
        near, pairs, counts = lax.optimization_barrier((near, localization_tile_pairs[0], used_pair_count[0]))
        return near, pair_lists(pairs, counts, tiles, obs_tiles)

    pieces, (entries, others) = gathered(mine, meanwhile)
    return filtered(entries, others, cell_coordinate, state, pieces)


def solution(mesh):
    placed = (
        P(("cell", "dp"), None),
        P(None, ("cell", "dp")),
        P("dp", "cell", None),
        P("dp", "cell"),
        P("dp", "cell"),
        P("dp", None, "cell"),
        P(("cell", "dp"), None, None, None),
        P(("cell", "dp"), None),
    )
    return jax.shard_map(
        local, mesh=mesh, in_specs=placed, out_specs=P(("cell", "dp"), None), check_vma=False
    )
```

```python
import functools
import math

import jax
import jax.numpy as jnp
from jax import lax
from jax.experimental import pallas as pl
from jax.experimental.pallas import tpu as pltpu
from jax.sharding import PartitionSpec as P

CT = 128
OBS_DEV = 128
EXTRA = 16
taper_rate = 2.0
LOG2E = math.log2(math.e)
GROUP = 8
AHEAD = 5
F32 = jnp.float32
BF16 = jnp.bfloat16
VMEM_LIMIT = 40 * 1024 * 1024


def in_vmem():
    return pl.BlockSpec(memory_space=pltpu.VMEM)


def in_smem():
    return pl.BlockSpec(memory_space=pltpu.SMEM)


def parts(x):
    hi = x.astype(BF16)
    rest = x - hi.astype(F32)
    mid = rest.astype(BF16)
    return hi, mid, (rest - mid.astype(F32)).astype(BF16)


def mm16(a, b):
    return jnp.dot(a, b, preferred_element_type=F32)


def mm_parts(a, b):
    def two(i, j, m, n):
        return mm16(jnp.concatenate([a[i], a[m]], axis=1), jnp.concatenate([b[j], b[n]], axis=0))

    return two(0, 0, 0, 1) + (two(1, 0, 0, 2) + two(1, 1, 2, 0))


def mm(a, b):
    return mm_parts(parts(a), parts(b))


def pack_kernel(pred, value, variance, coord, out):
    members = pred.shape[1]
    out[:members, :] = pred[...].astype(F32).T.astype(BF16)
    place = coord[...].astype(F32)
    lines = parts(value[...]) + parts(variance[...]) + tuple(place[j : j + 1] for j in range(3))
    out[members:, :] = stacked(lines).astype(BF16)


def pack(pred, value, variance, coord):
    return pl.pallas_call(
        pack_kernel,
        out_shape=jax.ShapeDtypeStruct((pred.shape[1] + EXTRA, pred.shape[0]), BF16),
        in_specs=[in_vmem()] * 4,
        out_specs=in_vmem(),
        name="pack_observations",
    )(pred, value, variance, coord)


def steps_of(size):
    return size.bit_length() - 1


def place_of(mask, size):
    steps = steps_of(size)
    return sum(((mask >> (steps - 1 - s)) & 1) << s for s in range(steps))


def swapped(block, axis, mask):
    return lax.ppermute(block, axis, [(i, i ^ mask) for i in range(lax.axis_size(axis))])


def gathered(mine, meanwhile):
    near = mine[None]
    for b in reversed(range(steps_of(lax.axis_size("cell")))):
        near = jnp.concatenate([near, swapped(near, "cell", 1 << b)], axis=0)
    near, work = meanwhile(near)
    pieces = {0: near}
    mask = lax.axis_size("dp") // 2
    while mask:
        for d in list(pieces):
            pieces[d ^ mask] = swapped(pieces[d], "dp", mask)
        if len(pieces) == 2:
            pieces[mask], work = lax.optimization_barrier((pieces[mask], work))
        mask //= 2
    return [pieces[d] for d in range(len(pieces))], work


def advanced(eye, rho, square, total):
    by = 1.0 / (2.0 - rho * rho)
    rest = rho * rho * by
    return rest, (2.0 * by) * square - rest * eye, (2.0 * by) * total


def series_start(eye, s):
    bound = jnp.max(jnp.sum(jnp.abs(s), axis=0, keepdims=True), axis=1, keepdims=True)
    bound = jnp.broadcast_to(bound, (1, s.shape[1]))
    scale = 2.0 / (2.0 + bound)
    r = eye - scale * (eye + s)
    return advanced(eye, bound / (2.0 + bound), mm(r, r), eye + r), scale


def series_step(eye, series):
    rho, r, total = series
    n = r.shape[0]
    pieces = parts(jnp.concatenate([r, total], axis=0))
    new = mm_parts(pieces, [p[:n] for p in pieces])
    return advanced(eye, rho, new[:n], total + new[n:])


def series_end(eye, series, both):
    rho, r, total = series
    n = r.shape[0]
    both[:n] = r
    both[n:] = total

    def more(carry):
        rho, left = carry
        return (rho > 6e-8) & (left > 0)

    def factor(carry):
        rho, left = carry
        rho, r, total = series_step(eye, (rho, both[:n], both[n:]))
        both[:n] = r
        both[n:] = total
        return rho, left - 1

    lax.while_loop(more, factor, (jnp.max(rho), jnp.int32(40)))
    return both[n:]


def stacked(lines):
    width = lines[0].shape[1]
    rows = lax.broadcasted_iota(jnp.int32, (16, width), 0)
    out = jnp.zeros((16, width), F32)
    for j, line in enumerate(lines):
        out = jnp.where(rows == j, line.astype(F32), out)
    return out


def norm_parts(place):
    return parts(-taper_rate * LOG2E * jnp.sum(place * place, axis=0, keepdims=True))


def cell_features(place):
    ones = [jnp.ones((1, place.shape[1]), F32)] * 3
    return stacked([place[j : j + 1] for j in range(3)] * 3 + list(norm_parts(place)) + ones)


def obs_features(place):
    ones = [jnp.ones((1, place.shape[1]), F32)] * 3
    scaled = parts(place * (2 * taper_rate * LOG2E))
    lines = [part[j : j + 1].astype(F32) for part in scaled for j in range(3)]
    return stacked(lines + ones + list(norm_parts(place))).astype(BF16)


def list_kernel(sizes_in, pairs, lists, *, tiles, obs_tiles):
    batches, _, slots = pairs.shape
    length = lists.shape[1]
    line = lax.broadcasted_iota(jnp.int32, (slots, slots), 1)
    down = lax.broadcasted_iota(jnp.int32, (slots, slots), 0)
    slot = lax.broadcasted_iota(jnp.int32, (slots, length), 1)

    def ones(mask, axis):
        return jnp.sum(jnp.where(mask, 1, 0), axis=axis, keepdims=True)

    row_codes = [pairs[k, 0:1, :] * obs_tiles + pairs[k, 1:2, :] for k in range(batches)]
    row_codes = jnp.concatenate(row_codes + [jnp.zeros((8 - batches, slots), jnp.int32)], axis=0)
    col_codes = row_codes.astype(F32).T.astype(jnp.int32)
    for k in range(batches):
        used = sizes_in[k]
        row = row_codes[k : k + 1]
        col = col_codes[:, k : k + 1]
        row = jnp.where(line[:1] < used, row, tiles * obs_tiles)
        col = jnp.where(down[:, :1] < used, col, tiles * obs_tiles)
        row_t, col_t = row // obs_tiles, col // obs_tiles
        same = row == col
        times = ones(same, 1)
        first_row = (ones(same & (down < line), 0) == 0) & (row_t < tiles)
        first_col = (ones(same & (line < down), 1) == 0) & (col_t < tiles)
        mates = row_t == col_t
        even_row = (ones(first_col & mates & (col < row), 0) & 1) == 0
        even_col = (ones(first_row & mates & (row < col), 1) & 1) == 0
        place = ones(first_row & even_row & (row <= col), 1) - 1
        here = first_col & (place == slot)
        value = ((col - col_t * obs_tiles) << 10) + times
        size = ones(first_row & even_row, 1)
        entry = jnp.sum(jnp.where(here & even_col, value + (col_t << 16), 0), axis=0, keepdims=True)
        other = jnp.sum(jnp.where(here & ~even_col, value, 0), axis=0, keepdims=True)
        lists[k : k + 1, :] = jnp.where(entry > 0, entry, tiles << 16)
        lists[batches + k : batches + k + 1, :] = jnp.where(slot[:1] == length - 1, size, other)


def pair_lists(pairs, counts, tiles, obs_tiles):
    batches, slots = pairs.shape[0], pairs.shape[2]
    length = -(-(slots + (AHEAD + 1) * GROUP) // 128) * 128
    return pl.pallas_call(
        functools.partial(list_kernel, tiles=tiles, obs_tiles=obs_tiles),
        out_shape=jax.ShapeDtypeStruct((2 * batches, length), jnp.int32),
        in_specs=[in_smem(), in_vmem()],
        out_specs=in_vmem(),
        cost_estimate=pl.CostEstimate(flops=40 * batches * slots * slots, bytes_accessed=16 * batches * slots, transcendentals=0),
        name="pair_lists",
    )(counts, pairs)


def filter_kernel(lists, coord, state, *refs, pieces_count):
    pieces, out, scratch = refs[:pieces_count], refs[pieces_count], refs[pieces_count + 1 :]
    blocks, ys, wd, of, gs, us, both_ref, bt, mp, prior, acc, pert, feat, held, tall, final, walk, where_cells, arrived, left = scratch
    batches, obs_tiles = of.shape[:2]
    members = state.shape[1]
    tiles = state.shape[0] // CT
    several = 4 if tiles % 4 == 0 else 1

    copies = [pltpu.make_async_copy(piece, blocks.at[d], arrived.at[d]) for d, piece in enumerate(pieces)]
    for n, (source, target) in enumerate(((coord, where_cells), (state, prior), (lists, walk))):
        copies.append(pltpu.make_async_copy(source, target, arrived.at[pieces_count + n]))
    for copy in copies:
        copy.start()

    rows = lax.broadcasted_iota(jnp.int32, (members, members), 0)
    cols = lax.broadcasted_iota(jnp.int32, (members, members), 1)
    eye = jnp.where(rows == cols, 1.0, 0.0)
    my_tile, my_batch = lax.axis_index("cell"), lax.axis_index("dp")

    copies[pieces_count].wait()
    tall[...] = cell_features(where_cells[...].astype(F32))
    acc[tiles] = jnp.zeros((CT, 2 * members), F32)
    pert[tiles] = jnp.zeros((CT, members), BF16)
    feat[tiles] = jnp.zeros((CT, 16), BF16)

    def over_tiles(body):
        def some(i, _):
            for j in range(several):
                body(i * several + j)
            return 0

        lax.fori_loop(0, tiles // several, some, 0)

    def describe(t):
        feat[t] = tall[:, pl.ds(pl.multiple_of(t * CT, CT), CT)].T.astype(BF16)

    over_tiles(describe)

    for rd in range(batches):
        copies[rd].wait()
        lefts, rights = [], []
        k = my_batch ^ rd
        for rc in range(obs_tiles):
            u = my_tile ^ rc
            r = place_of(rc, obs_tiles)
            raw = blocks[rd, r, :members, :]
            y = raw.astype(F32)
            e = blocks[rd, r, members:, :].astype(F32)
            value = e[0:1] + e[1:2] + e[2:3]
            variance = e[3:4] + e[4:5] + e[5:6]
            mean = jnp.mean(y, axis=0, keepdims=True)
            w = 1.0 / variance
            where = pl.ds(pl.multiple_of(u * OBS_DEV, OBS_DEV), OBS_DEV)
            ys[k, :, where] = raw
            wd[k, 0:1, where] = w
            wd[k, 1:2, where] = value
            of[k, u] = obs_features(e[6:9])
            z = jnp.broadcast_to((value - mean) * w, (16, OBS_DEV))
            lefts.append(parts(jnp.concatenate([(y - mean) * w, z], axis=0)))
            rights.append(raw)
        right = jnp.concatenate(rights, axis=1)
        g = sum(
            lax.dot_general(
                jnp.concatenate(part, axis=1), right, (((1,), (1,)), ((), ())), preferred_element_type=F32
            )
            for part in zip(*lefts)
        )
        g = g - jnp.mean(g, axis=1, keepdims=True)
        gs[k] = g[:members]
        us[k] = g[members:]

    copies[pieces_count + 1].wait()
    copies[pieces_count + 2].wait()

    def prepare(t):
        x = prior[pl.ds(pl.multiple_of(t * CT, CT), CT), :].astype(F32)
        acc[t, :, :members] = x
        acc[t, :, members:] = x - jnp.mean(x, axis=1, keepdims=True)

    over_tiles(prepare)

    qt = eye - 1.0 / members
    p = jnp.full((16, members), 1.0 / members, F32)
    chunk = min(2, obs_tiles) * OBS_DEV
    series, scale = series_start(eye, gs[0] * (1.0 / (members - 1)))
    for _ in range(3):
        series = series_step(eye, series)
    for k in range(batches):
        inverse = scale * series_end(eye, series, both_ref)
        inverse_parts = parts(inverse)
        qt_parts = parts(qt)
        mt = mm_parts(inverse_parts, qt_parts)
        ht = 0.5 * qt + p[0:1]
        hi, mid, lo = parts(jnp.concatenate([mt, ht], axis=0))
        twice = jnp.concatenate([hi, mid], axis=1)
        for n in range(obs_tiles * OBS_DEV // chunk):
            where = pl.ds(n * chunk, chunk)
            y = ys[k, :, where]
            both = mm16(twice, jnp.concatenate([y, y], axis=0)) + mm16(lo, y)
            b = (both[:members] * (1.0 / (members - 1))).astype(BF16)
            pull = wd[k, 0:1, where] * (wd[k, 1:2, where] - both[members:])
            pulls = jnp.concatenate([pull, pull - jnp.mean(pull, axis=0, keepdims=True)], axis=0).astype(BF16)
            for c in range(chunk // OBS_DEV):
                u = n * (chunk // OBS_DEV) + c
                bt[u] = b[:, c * OBS_DEV : (c + 1) * OBS_DEV]
                mp[u] = pulls[:, c * OBS_DEV : (c + 1) * OBS_DEV].T
        if k + 1 < batches:
            half = parts(0.5 * (eye + inverse))
            step = parts(mm_parts(parts(us[k]), inverse_parts) * (1.0 / (members - 1)))
            p = p + mm_parts(step, qt_parts)
            qt = 0.5 * (qt + mt)

        def change_basis(j):
            g_j = parts(gs[j])
            gs[j] = mm_parts(half, parts(mm_parts(g_j, half)))
            us[j] = mm_parts(parts(us[j] - mm_parts(step, g_j)), half)

        def centre(t):
            pert[t] = acc[t, :, members:].astype(BF16)

        over_tiles(centre)

        def named(i, j):
            e, o = walk[k, i * GROUP + j], walk[batches + k, i * GROUP + j]
            return e >> 16, (e >> 10) & 63, o >> 10, e & 1023, o & 1023

        def weigh(i):
            for j in range(GROUP):
                t, u0, u1, m0, m1 = named(i, j)
                score = mm16(pert[t], jnp.concatenate([bt[u0], bt[u1]], axis=1))
                power = mm16(feat[t], jnp.concatenate([of[k, u0], of[k, u1]], axis=1))
                taper = jnp.exp2(power)
                for n, m in enumerate((m0, m1)):
                    cut = slice(n * OBS_DEV, (n + 1) * OBS_DEV)
                    held[j, :, cut] = (taper[:, cut] * (score[:, cut] * m.astype(F32))).astype(BF16)

        def draw(i):
            for j in range(GROUP):
                t, u0, u1, _, _ = named(i, j)
                acc[t] += mm16(held[j], jnp.concatenate([mp[u0], mp[u1]], axis=0))

        def group(i, _):
            draw(i - 1)
            weigh(i)
            return 0

        groups = (walk[batches + k, walk.shape[1] - 1] + GROUP - 1) // GROUP
        weigh(0)
        if k + 1 < batches:
            change_basis(k + 1)
            for i in range(1, AHEAD):
                draw(i - 1)
                if i == 1:
                    series, scale = series_start(eye, gs[k + 1] * (1.0 / (members - 1)))
                else:
                    series = series_step(eye, series)
                if k + 1 + i < batches:
                    change_basis(k + 1 + i)
                weigh(i)
            groups = jnp.maximum(groups, AHEAD)
            lax.fori_loop(AHEAD, groups, group, 0)
        else:
            lax.fori_loop(1, groups, group, 0)
        draw(groups - 1)

    leaving = []
    for n in range(left.shape[0]):
        share = tiles // left.shape[0]

        def finish(i, _):
            t = n * share + i
            final[pl.ds(pl.multiple_of(t * CT, CT), CT), :] = acc[t, :, :members].astype(BF16)
            return 0

        lax.fori_loop(0, share, finish, 0)
        where = pl.ds(n * share * CT, share * CT)
        leaving.append(pltpu.make_async_copy(final.at[where], out.at[where], left.at[n]))
        leaving[-1].start()
    for copy in leaving:
        copy.wait()


def filtered(lists, coord, state, pieces):
    batches = len(pieces)
    obs_tiles, rows = pieces[0].shape[:2]
    members = state.shape[1]
    tiles = state.shape[0] // CT
    shares = 4 if tiles % 4 == 0 else 1
    anywhere = pl.BlockSpec(memory_space=pl.ANY)
    return pl.pallas_call(
        functools.partial(filter_kernel, pieces_count=batches),
        out_shape=jax.ShapeDtypeStruct(state.shape, BF16),
        in_specs=[pl.BlockSpec(memory_space=pltpu.HBM)] * 3 + [anywhere] * batches,
        out_specs=anywhere,
        scratch_shapes=[
            pltpu.VMEM((batches, obs_tiles, rows, OBS_DEV), BF16),
            pltpu.VMEM((batches, members, obs_tiles * OBS_DEV), BF16),
            pltpu.VMEM((batches, 8, obs_tiles * OBS_DEV), F32),
            pltpu.VMEM((batches, obs_tiles, 16, OBS_DEV), BF16),
            pltpu.VMEM((batches, members, members), F32),
            pltpu.VMEM((batches, 16, members), F32),
            pltpu.VMEM((2 * members, members), F32),
            pltpu.VMEM((obs_tiles, members, OBS_DEV), BF16),
            pltpu.VMEM((obs_tiles, OBS_DEV, 2 * members), BF16),
            pltpu.VMEM(state.shape, BF16),
            pltpu.VMEM((tiles + 1, CT, 2 * members), F32),
            pltpu.VMEM((tiles + 1, CT, members), BF16),
            pltpu.VMEM((tiles + 1, CT, 16), BF16),
            pltpu.VMEM((GROUP, CT, 2 * OBS_DEV), BF16),
            pltpu.VMEM((16, tiles * CT), F32),
            pltpu.VMEM(state.shape, BF16),
            pltpu.SMEM(lists.shape, jnp.int32),
            pltpu.VMEM(coord.shape, BF16),
            pltpu.SemaphoreType.DMA((batches + 3,)),
            pltpu.SemaphoreType.DMA((shares,)),
        ],
        compiler_params=pltpu.CompilerParams(vmem_limit_bytes=VMEM_LIMIT),
        name="filter",
    )(lists, coord, state, *pieces)


def local(
    state,
    cell_coordinate,
    member_predictions,
    measured_values,
    obs_error_variance,
    observation_coordinate,
    localization_tile_pairs,
    used_pair_count,
):
    obs_tiles = lax.axis_size("cell")
    batches = lax.axis_size("dp")
    tiles = state.shape[0] // CT
    mine = pack(member_predictions[0], measured_values, obs_error_variance, observation_coordinate[0])

    def meanwhile(near):
        near, pairs, counts = lax.optimization_barrier((near, localization_tile_pairs[0], used_pair_count[0]))
        return near, pair_lists(pairs, counts, tiles, obs_tiles)

    pieces, lists = gathered(mine, meanwhile)
    return filtered(lists, cell_coordinate, state, pieces)


def solution(mesh):
    placed = (
        P(("cell", "dp"), None),
        P(None, ("cell", "dp")),
        P("dp", "cell", None),
        P("dp", "cell"),
        P("dp", "cell"),
        P("dp", None, "cell"),
        P(("cell", "dp"), None, None, None),
        P(("cell", "dp"), None),
    )
    return jax.shard_map(
        local, mesh=mesh, in_specs=placed, out_specs=P(("cell", "dp"), None), check_vma=False
    )
```

```python
import functools
import math

import jax
import jax.numpy as jnp
from jax import lax
from jax.experimental import pallas as pl
from jax.experimental.pallas import tpu as pltpu
from jax.sharding import PartitionSpec as P

CT = 128
OBS_DEV = 128
EXTRA = 16
taper_rate = 2.0
LOG2E = math.log2(math.e)
GROUP = 8
AHEAD = 5
F32 = jnp.float32
BF16 = jnp.bfloat16
VMEM_LIMIT = 40 * 1024 * 1024


def in_vmem():
    return pl.BlockSpec(memory_space=pltpu.VMEM)


def in_smem():
    return pl.BlockSpec(memory_space=pltpu.SMEM)


def parts(x):
    hi = x.astype(BF16)
    rest = x - hi.astype(F32)
    mid = rest.astype(BF16)
    return hi, mid, (rest - mid.astype(F32)).astype(BF16)


def mm16(a, b):
    return jnp.dot(a, b, preferred_element_type=F32)


def mm_parts(a, b):
    def two(i, j, m, n):
        return mm16(jnp.concatenate([a[i], a[m]], axis=1), jnp.concatenate([b[j], b[n]], axis=0))

    return two(0, 0, 0, 1) + (two(1, 0, 0, 2) + two(1, 1, 2, 0))


def mm(a, b):
    return mm_parts(parts(a), parts(b))


def pack_kernel(pred, value, variance, coord, out):
    members = pred.shape[1]
    out[:members, :] = pred[...].astype(F32).T.astype(BF16)
    place = coord[...].astype(F32)
    lines = parts(value[...]) + parts(variance[...]) + tuple(place[j : j + 1] for j in range(3))
    out[members:, :] = stacked(lines).astype(BF16)


def pack(pred, value, variance, coord):
    return pl.pallas_call(
        pack_kernel,
        out_shape=jax.ShapeDtypeStruct((pred.shape[1] + EXTRA, pred.shape[0]), BF16),
        in_specs=[in_vmem()] * 4,
        out_specs=in_vmem(),
        name="pack_observations",
    )(pred, value, variance, coord)


def steps_of(size):
    return size.bit_length() - 1


def place_of(mask, size):
    steps = steps_of(size)
    return sum(((mask >> (steps - 1 - s)) & 1) << s for s in range(steps))


def swapped(block, axis, mask):
    return lax.ppermute(block, axis, [(i, i ^ mask) for i in range(lax.axis_size(axis))])


def gathered(mine, jobs):
    near, results = mine[None], []

    def beside(near, axis, mask):
        if not jobs:
            return swapped(near, axis, mask)
        job, arguments = jobs.pop(0)
        near, arguments = lax.optimization_barrier((near, arguments))
        far, result = lax.optimization_barrier((swapped(near, axis, mask), job(*arguments)))
        results.append(result)
        return far

    steps = steps_of(lax.axis_size("cell"))
    for b in reversed(range(steps)):
        far = beside(near, "cell", 1 << b) if b + 1 < len(jobs) else swapped(near, "cell", 1 << b)
        near = jnp.concatenate([near, far], axis=0)
    pieces = {0: near}
    mask = lax.axis_size("dp") // 2
    while mask:
        for d in list(pieces):
            pieces[d ^ mask] = beside(pieces[d], "dp", mask)
        mask //= 2
    return [pieces[d] for d in range(len(pieces))], results


def advanced(eye, rho, square, total):
    by = 1.0 / (2.0 - rho * rho)
    rest = rho * rho * by
    return rest, (2.0 * by) * square - rest * eye, (2.0 * by) * total


def series_start(eye, s):
    bound = jnp.max(jnp.sum(jnp.abs(s), axis=0, keepdims=True), axis=1, keepdims=True)
    bound = jnp.broadcast_to(bound, (1, s.shape[1]))
    scale = 2.0 / (2.0 + bound)
    r = eye - scale * (eye + s)
    return advanced(eye, bound / (2.0 + bound), mm(r, r), eye + r), scale


def series_step(eye, series):
    rho, r, total = series
    n = r.shape[0]
    pieces = parts(jnp.concatenate([r, total], axis=0))
    new = mm_parts(pieces, [p[:n] for p in pieces])
    return advanced(eye, rho, new[:n], total + new[n:])


def series_end(eye, series, both):
    rho, r, total = series
    n = r.shape[0]
    both[:n] = r
    both[n:] = total

    def more(carry):
        rho, left = carry
        return (rho > 6e-8) & (left > 0)

    def factor(carry):
        rho, left = carry
        rho, r, total = series_step(eye, (rho, both[:n], both[n:]))
        both[:n] = r
        both[n:] = total
        return rho, left - 1

    lax.while_loop(more, factor, (jnp.max(rho), jnp.int32(40)))
    return both[n:]


def stacked(lines):
    width = lines[0].shape[1]
    rows = lax.broadcasted_iota(jnp.int32, (16, width), 0)
    out = jnp.zeros((16, width), F32)
    for j, line in enumerate(lines):
        out = jnp.where(rows == j, line.astype(F32), out)
    return out


def norm_parts(place):
    return parts(-taper_rate * LOG2E * jnp.sum(place * place, axis=0, keepdims=True))


def cell_features(place):
    ones = [jnp.ones((1, place.shape[1]), F32)] * 3
    return stacked([place[j : j + 1] for j in range(3)] * 3 + list(norm_parts(place)) + ones)


def obs_features(place):
    ones = [jnp.ones((1, place.shape[1]), F32)] * 3
    scaled = parts(place * (2 * taper_rate * LOG2E))
    lines = [part[j : j + 1].astype(F32) for part in scaled for j in range(3)]
    return stacked(lines + ones + list(norm_parts(place))).astype(BF16)


def list_kernel(sizes_in, pairs, lists, *, tiles, obs_tiles):
    batches, _, slots = pairs.shape
    length = lists.shape[1]
    line = lax.broadcasted_iota(jnp.int32, (slots, slots), 1)
    down = lax.broadcasted_iota(jnp.int32, (slots, slots), 0)
    slot = lax.broadcasted_iota(jnp.int32, (slots, length), 1)

    def ones(mask, axis):
        return jnp.sum(jnp.where(mask, 1, 0), axis=axis, keepdims=True)

    row_codes = [pairs[k, 0:1, :] * obs_tiles + pairs[k, 1:2, :] for k in range(batches)]
    row_codes = jnp.concatenate(row_codes + [jnp.zeros((8 - batches, slots), jnp.int32)], axis=0)
    col_codes = row_codes.astype(F32).T.astype(jnp.int32)
    for k in range(batches):
        used = sizes_in[k]
        row = row_codes[k : k + 1]
        col = col_codes[:, k : k + 1]
        row = jnp.where(line[:1] < used, row, tiles * obs_tiles)
        col = jnp.where(down[:, :1] < used, col, tiles * obs_tiles)
        row_t, col_t = row // obs_tiles, col // obs_tiles
        same = row == col
        times = ones(same, 1)
        first_row = (ones(same & (down < line), 0) == 0) & (row_t < tiles)
        first_col = (ones(same & (line < down), 1) == 0) & (col_t < tiles)
        mates = row_t == col_t
        even_row = (ones(first_col & mates & (col < row), 0) & 1) == 0
        even_col = (ones(first_row & mates & (row < col), 1) & 1) == 0
        place = ones(first_row & even_row & (row <= col), 1) - 1
        here = first_col & (place == slot)
        value = ((col - col_t * obs_tiles) << 10) + times
        size = ones(first_row & even_row, 1)
        entry = jnp.sum(jnp.where(here & even_col, value + (col_t << 16), 0), axis=0, keepdims=True)
        other = jnp.sum(jnp.where(here & ~even_col, value, 0), axis=0, keepdims=True)
        lists[k : k + 1, :] = jnp.where(entry > 0, entry, tiles << 16)
        lists[batches + k : batches + k + 1, :] = jnp.where(slot[:1] == length - 1, size, other)


def pair_lists(pairs, counts, tiles, obs_tiles):
    batches, slots = pairs.shape[0], pairs.shape[2]
    length = -(-(slots + (AHEAD + 1) * GROUP) // 128) * 128
    return pl.pallas_call(
        functools.partial(list_kernel, tiles=tiles, obs_tiles=obs_tiles),
        out_shape=jax.ShapeDtypeStruct((2 * batches, length), jnp.int32),
        in_specs=[in_smem(), in_vmem()],
        out_specs=in_vmem(),
        cost_estimate=pl.CostEstimate(flops=40 * batches * slots * slots, bytes_accessed=16 * batches * slots, transcendentals=0),
        name="pair_lists",
    )(counts, pairs)


def feature_kernel(coord, feat, tall):
    tall[...] = cell_features(coord[...].astype(F32))
    for t in range(feat.shape[0]):
        feat[t] = tall[:, t * CT : (t + 1) * CT].T.astype(BF16)


def features(coord):
    cells = coord.shape[1]
    return pl.pallas_call(
        feature_kernel,
        out_shape=jax.ShapeDtypeStruct((cells // CT, CT, 16), BF16),
        in_specs=[in_vmem()],
        out_specs=in_vmem(),
        scratch_shapes=[pltpu.VMEM((16, cells), F32)],
        cost_estimate=pl.CostEstimate(flops=300 * cells, bytes_accessed=300 * cells, transcendentals=0),
        name="cell_features",
    )(coord)


def centre_kernel(state, work):
    members = state.shape[1]
    for t in range(work.shape[0]):
        x = state[t * CT : (t + 1) * CT, :].astype(F32)
        work[t, :, :members] = x
        work[t, :, members:] = x - jnp.mean(x, axis=1, keepdims=True)


def centred(state):
    cells, members = state.shape
    tiles = cells // CT
    share = 8 if tiles % 8 == 0 else 1
    return pl.pallas_call(
        centre_kernel,
        out_shape=jax.ShapeDtypeStruct((tiles, CT, 2 * members), F32),
        grid=(tiles // share,),
        in_specs=[pl.BlockSpec((share * CT, members), lambda i: (i, 0))],
        out_specs=pl.BlockSpec((share, CT, 2 * members), lambda i: (i, 0, 0)),
        cost_estimate=pl.CostEstimate(flops=4 * cells * members, bytes_accessed=10 * cells * members, transcendentals=0),
        name="centred_state",
    )(state)


def filter_kernel(lists, cell_lines, work, *refs, pieces_count):
    pieces, out, scratch = refs[:pieces_count], refs[pieces_count], refs[pieces_count + 1 :]
    blocks, ys, wd, of, gs, us, both_ref, bt, mp, acc, pert, feat, held, final, walk, arrived, left = scratch
    batches, obs_tiles = of.shape[:2]
    tiles, _, members = pert.shape
    tiles -= 1
    several = 4 if tiles % 4 == 0 else 1

    copies = [pltpu.make_async_copy(piece, blocks.at[d], arrived.at[d]) for d, piece in enumerate(pieces)]
    own = pl.ds(0, tiles)
    for n, (source, target) in enumerate(((lists, walk), (cell_lines, feat.at[own]), (work, acc.at[own]))):
        copies.append(pltpu.make_async_copy(source, target, arrived.at[pieces_count + n]))
    for copy in copies:
        copy.start()

    rows = lax.broadcasted_iota(jnp.int32, (members, members), 0)
    cols = lax.broadcasted_iota(jnp.int32, (members, members), 1)
    eye = jnp.where(rows == cols, 1.0, 0.0)
    my_tile, my_batch = lax.axis_index("cell"), lax.axis_index("dp")

    acc[tiles] = jnp.zeros((CT, 2 * members), F32)
    pert[tiles] = jnp.zeros((CT, members), BF16)
    feat[tiles] = jnp.zeros((CT, 16), BF16)

    def over_tiles(body):
        def some(i, _):
            for j in range(several):
                body(i * several + j)
            return 0

        lax.fori_loop(0, tiles // several, some, 0)

    for rd in range(batches):
        copies[rd].wait()
        lefts, rights = [], []
        k = my_batch ^ rd
        for rc in range(obs_tiles):
            u = my_tile ^ rc
            r = place_of(rc, obs_tiles)
            raw = blocks[rd, r, :members, :]
            y = raw.astype(F32)
            e = blocks[rd, r, members:, :].astype(F32)
            value = e[0:1] + e[1:2] + e[2:3]
            variance = e[3:4] + e[4:5] + e[5:6]
            mean = jnp.mean(y, axis=0, keepdims=True)
            w = 1.0 / variance
            where = pl.ds(pl.multiple_of(u * OBS_DEV, OBS_DEV), OBS_DEV)
            ys[k, :, where] = raw
            wd[k, 0:1, where] = w
            wd[k, 1:2, where] = value
            of[k, u] = obs_features(e[6:9])
            z = jnp.broadcast_to((value - mean) * w, (16, OBS_DEV))
            lefts.append(parts(jnp.concatenate([(y - mean) * w, z], axis=0)))
            rights.append(raw)
        right = jnp.concatenate(rights, axis=1)
        g = sum(
            lax.dot_general(
                jnp.concatenate(part, axis=1), right, (((1,), (1,)), ((), ())), preferred_element_type=F32
            )
            for part in zip(*lefts)
        )
        g = g - jnp.mean(g, axis=1, keepdims=True)
        gs[k] = g[:members]
        us[k] = g[members:]

    qt = eye - 1.0 / members
    p = jnp.full((16, members), 1.0 / members, F32)
    chunk = min(2, obs_tiles) * OBS_DEV
    series, scale = series_start(eye, gs[0] * (1.0 / (members - 1)))
    for _ in range(3):
        series = series_step(eye, series)
    for k in range(batches):
        inverse = scale * series_end(eye, series, both_ref)
        inverse_parts = parts(inverse)
        qt_parts = parts(qt)
        mt = mm_parts(inverse_parts, qt_parts)
        ht = 0.5 * qt + p[0:1]
        hi, mid, lo = parts(jnp.concatenate([mt, ht], axis=0))
        twice = jnp.concatenate([hi, mid], axis=1)
        for n in range(obs_tiles * OBS_DEV // chunk):
            where = pl.ds(n * chunk, chunk)
            y = ys[k, :, where]
            both = mm16(twice, jnp.concatenate([y, y], axis=0)) + mm16(lo, y)
            b = (both[:members] * (1.0 / (members - 1))).astype(BF16)
            pull = wd[k, 0:1, where] * (wd[k, 1:2, where] - both[members:])
            pulls = jnp.concatenate([pull, pull - jnp.mean(pull, axis=0, keepdims=True)], axis=0).astype(BF16)
            for c in range(chunk // OBS_DEV):
                u = n * (chunk // OBS_DEV) + c
                bt[u] = b[:, c * OBS_DEV : (c + 1) * OBS_DEV]
                mp[u] = pulls[:, c * OBS_DEV : (c + 1) * OBS_DEV].T
        if k + 1 < batches:
            half = parts(0.5 * (eye + inverse))
            step = parts(mm_parts(parts(us[k]), inverse_parts) * (1.0 / (members - 1)))
            p = p + mm_parts(step, qt_parts)
            qt = 0.5 * (qt + mt)

        def change_basis(j):
            g_j = parts(gs[j])
            gs[j] = mm_parts(half, parts(mm_parts(g_j, half)))
            us[j] = mm_parts(parts(us[j] - mm_parts(step, g_j)), half)

        if k == 0:
            for copy in copies[pieces_count:]:
                copy.wait()

        def centre(t):
            pert[t] = acc[t, :, members:].astype(BF16)

        over_tiles(centre)

        def named(i, j):
            e, o = walk[k, i * GROUP + j], walk[batches + k, i * GROUP + j]
            return e >> 16, (e >> 10) & 63, o >> 10, e & 1023, o & 1023

        def weigh(i):
            for j in range(GROUP):
                t, u0, u1, m0, m1 = named(i, j)
                score = mm16(pert[t], jnp.concatenate([bt[u0], bt[u1]], axis=1))
                power = mm16(feat[t], jnp.concatenate([of[k, u0], of[k, u1]], axis=1))
                taper = jnp.exp2(power)
                for n, m in enumerate((m0, m1)):
                    cut = slice(n * OBS_DEV, (n + 1) * OBS_DEV)
                    held[j, :, cut] = (taper[:, cut] * (score[:, cut] * m.astype(F32))).astype(BF16)

        def draw(i):
            for j in range(GROUP):
                t, u0, u1, _, _ = named(i, j)
                acc[t] += mm16(held[j], jnp.concatenate([mp[u0], mp[u1]], axis=0))

        def group(i, _):
            draw(i - 1)
            weigh(i)
            return 0

        groups = (walk[batches + k, walk.shape[1] - 1] + GROUP - 1) // GROUP
        weigh(0)
        if k + 1 < batches:
            change_basis(k + 1)
            for i in range(1, AHEAD):
                draw(i - 1)
                if i == 1:
                    series, scale = series_start(eye, gs[k + 1] * (1.0 / (members - 1)))
                else:
                    series = series_step(eye, series)
                if k + 1 + i < batches:
                    change_basis(k + 1 + i)
                weigh(i)
            groups = jnp.maximum(groups, AHEAD)
            lax.fori_loop(AHEAD, groups, group, 0)
        else:
            lax.fori_loop(1, groups, group, 0)
        draw(groups - 1)

    leaving = []
    for n in range(left.shape[0]):
        share = tiles // left.shape[0]

        def finish(i, _):
            t = n * share + i
            final[pl.ds(pl.multiple_of(t * CT, CT), CT), :] = acc[t, :, :members].astype(BF16)
            return 0

        lax.fori_loop(0, share, finish, 0)
        where = pl.ds(n * share * CT, share * CT)
        leaving.append(pltpu.make_async_copy(final.at[where], out.at[where], left.at[n]))
        leaving[-1].start()
    for copy in leaving:
        copy.wait()


def filtered(lists, cell_lines, work, pieces):
    batches = len(pieces)
    obs_tiles, rows = pieces[0].shape[:2]
    tiles = work.shape[0]
    members = work.shape[2] // 2
    cells = tiles * CT
    shares = 4 if tiles % 4 == 0 else 1
    anywhere = pl.BlockSpec(memory_space=pl.ANY)
    return pl.pallas_call(
        functools.partial(filter_kernel, pieces_count=batches),
        out_shape=jax.ShapeDtypeStruct((cells, members), BF16),
        in_specs=[anywhere] * (3 + batches),
        out_specs=anywhere,
        scratch_shapes=[
            pltpu.VMEM((batches, obs_tiles, rows, OBS_DEV), BF16),
            pltpu.VMEM((batches, members, obs_tiles * OBS_DEV), BF16),
            pltpu.VMEM((batches, 8, obs_tiles * OBS_DEV), F32),
            pltpu.VMEM((batches, obs_tiles, 16, OBS_DEV), BF16),
            pltpu.VMEM((batches, members, members), F32),
            pltpu.VMEM((batches, 16, members), F32),
            pltpu.VMEM((2 * members, members), F32),
            pltpu.VMEM((obs_tiles, members, OBS_DEV), BF16),
            pltpu.VMEM((obs_tiles, OBS_DEV, 2 * members), BF16),
            pltpu.VMEM((tiles + 1, CT, 2 * members), F32),
            pltpu.VMEM((tiles + 1, CT, members), BF16),
            pltpu.VMEM((tiles + 1, CT, 16), BF16),
            pltpu.VMEM((GROUP, CT, 2 * OBS_DEV), BF16),
            pltpu.VMEM((cells, members), BF16),
            pltpu.SMEM(lists.shape, jnp.int32),
            pltpu.SemaphoreType.DMA((batches + 3,)),
            pltpu.SemaphoreType.DMA((shares,)),
        ],
        compiler_params=pltpu.CompilerParams(vmem_limit_bytes=VMEM_LIMIT),
        name="filter",
    )(lists, cell_lines, work, *pieces)


def local(
    state,
    cell_coordinate,
    member_predictions,
    measured_values,
    obs_error_variance,
    observation_coordinate,
    localization_tile_pairs,
    used_pair_count,
):
    obs_tiles = lax.axis_size("cell")
    batches = lax.axis_size("dp")
    tiles = state.shape[0] // CT
    mine = pack(member_predictions[0], measured_values, obs_error_variance, observation_coordinate[0])

    jobs = [
        (features, (cell_coordinate,)),
        (centred, (state,)),
        (
            functools.partial(pair_lists, tiles=tiles, obs_tiles=obs_tiles),
            (localization_tile_pairs[0], used_pair_count[0]),
        ),
    ]
    pieces, (cell_lines, work, lists) = gathered(mine, jobs)
    return filtered(lists, cell_lines, work, pieces)


def solution(mesh):
    placed = (
        P(("cell", "dp"), None),
        P(None, ("cell", "dp")),
        P("dp", "cell", None),
        P("dp", "cell"),
        P("dp", "cell"),
        P("dp", None, "cell"),
        P(("cell", "dp"), None, None, None),
        P(("cell", "dp"), None),
    )
    return jax.shard_map(
        local, mesh=mesh, in_specs=placed, out_specs=P(("cell", "dp"), None), check_vma=False
    )
```

```python
import functools
import math

import jax
import jax.numpy as jnp
from jax import lax
from jax.experimental import pallas as pl
from jax.experimental.pallas import tpu as pltpu
from jax.sharding import PartitionSpec as P

CT = 128
OBS_DEV = 128
EXTRA = 16
taper_rate = 2.0
LOG2E = math.log2(math.e)
GROUP = 8
AHEAD = 5
F32 = jnp.float32
BF16 = jnp.bfloat16
VMEM_LIMIT = 60 * 1024 * 1024


def in_vmem():
    return pl.BlockSpec(memory_space=pltpu.VMEM)


def in_smem():
    return pl.BlockSpec(memory_space=pltpu.SMEM)


def parts(x):
    hi = x.astype(BF16)
    rest = x - hi.astype(F32)
    mid = rest.astype(BF16)
    return hi, mid, (rest - mid.astype(F32)).astype(BF16)


def mm16(a, b):
    return jnp.dot(a, b, preferred_element_type=F32)


def mm_parts(a, b):
    def two(i, j, m, n):
        return mm16(jnp.concatenate([a[i], a[m]], axis=1), jnp.concatenate([b[j], b[n]], axis=0))

    return two(0, 0, 0, 1) + (two(1, 0, 0, 2) + two(1, 1, 2, 0))


def mm(a, b):
    return mm_parts(parts(a), parts(b))


def pack_kernel(pred, value, variance, coord, out):
    members = pred.shape[1]
    out[:members, :] = pred[...].astype(F32).T.astype(BF16)
    place = coord[...].astype(F32)
    lines = parts(value[...]) + parts(variance[...]) + tuple(place[j : j + 1] for j in range(3))
    out[members:, :] = stacked(lines).astype(BF16)


def pack(pred, value, variance, coord):
    return pl.pallas_call(
        pack_kernel,
        out_shape=jax.ShapeDtypeStruct((pred.shape[1] + EXTRA, pred.shape[0]), BF16),
        in_specs=[in_vmem()] * 4,
        out_specs=in_vmem(),
        name="pack_observations",
    )(pred, value, variance, coord)


def steps_of(size):
    return size.bit_length() - 1


def place_of(mask, size):
    steps = steps_of(size)
    return sum(((mask >> (steps - 1 - s)) & 1) << s for s in range(steps))


def swapped(block, axis, mask):
    return lax.ppermute(block, axis, [(i, i ^ mask) for i in range(lax.axis_size(axis))])


def gathered(mine, jobs):
    near, results = mine[None], []

    def beside(near, axis, mask):
        if not jobs:
            return swapped(near, axis, mask)
        job, arguments = jobs.pop(0)
        near, arguments = lax.optimization_barrier((near, arguments))
        far, result = lax.optimization_barrier((swapped(near, axis, mask), job(*arguments)))
        results.append(result)
        return far

    steps = steps_of(lax.axis_size("cell"))
    for b in reversed(range(steps)):
        far = beside(near, "cell", 1 << b) if b + 1 < len(jobs) else swapped(near, "cell", 1 << b)
        near = jnp.concatenate([near, far], axis=0)
    pieces = {0: near}
    mask = lax.axis_size("dp") // 2
    while mask:
        for d in list(pieces):
            pieces[d ^ mask] = beside(pieces[d], "dp", mask)
        mask //= 2
    return [pieces[d] for d in range(len(pieces))], results


def advanced(eye, rho, square, total):
    by = 1.0 / (2.0 - rho * rho)
    rest = rho * rho * by
    return rest, (2.0 * by) * square - rest * eye, (2.0 * by) * total


def series_start(eye, s):
    bound = jnp.max(jnp.sum(jnp.abs(s), axis=0, keepdims=True), axis=1, keepdims=True)
    bound = jnp.broadcast_to(bound, (1, s.shape[1]))
    scale = 2.0 / (2.0 + bound)
    r = eye - scale * (eye + s)
    return advanced(eye, bound / (2.0 + bound), mm(r, r), eye + r), scale


def series_step(eye, series):
    rho, r, total = series
    n = r.shape[0]
    pieces = parts(jnp.concatenate([r, total], axis=0))
    new = mm_parts(pieces, [p[:n] for p in pieces])
    return advanced(eye, rho, new[:n], total + new[n:])


def series_end(eye, series, both):
    rho, r, total = series
    n = r.shape[0]
    both[:n] = r
    both[n:] = total

    def more(carry):
        rho, left = carry
        return (rho > 6e-8) & (left > 0)

    def factor(carry):
        rho, left = carry
        rho, r, total = series_step(eye, (rho, both[:n], both[n:]))
        both[:n] = r
        both[n:] = total
        return rho, left - 1

    lax.while_loop(more, factor, (jnp.max(rho), jnp.int32(40)))
    return both[n:]


def stacked(lines):
    width = lines[0].shape[1]
    rows = lax.broadcasted_iota(jnp.int32, (16, width), 0)
    out = jnp.zeros((16, width), F32)
    for j, line in enumerate(lines):
        out = jnp.where(rows == j, line.astype(F32), out)
    return out


def norm_parts(place):
    return parts(-taper_rate * LOG2E * jnp.sum(place * place, axis=0, keepdims=True))


def cell_features(place):
    ones = [jnp.ones((1, place.shape[1]), F32)] * 3
    return stacked([place[j : j + 1] for j in range(3)] * 3 + list(norm_parts(place)) + ones)


def obs_features(place):
    ones = [jnp.ones((1, place.shape[1]), F32)] * 3
    scaled = parts(place * (2 * taper_rate * LOG2E))
    lines = [part[j : j + 1].astype(F32) for part in scaled for j in range(3)]
    return stacked(lines + ones + list(norm_parts(place))).astype(BF16)


def list_kernel(sizes_in, pairs, lists, *, tiles, obs_tiles):
    batches, _, slots = pairs.shape
    length = lists.shape[1]
    line = lax.broadcasted_iota(jnp.int32, (slots, slots), 1)
    down = lax.broadcasted_iota(jnp.int32, (slots, slots), 0)
    slot = lax.broadcasted_iota(jnp.int32, (slots, length), 1)

    def ones(mask, axis):
        return jnp.sum(jnp.where(mask, 1, 0), axis=axis, keepdims=True)

    row_codes = [pairs[k, 0:1, :] * obs_tiles + pairs[k, 1:2, :] for k in range(batches)]
    row_codes = jnp.concatenate(row_codes + [jnp.zeros((8 - batches, slots), jnp.int32)], axis=0)
    col_codes = row_codes.astype(F32).T.astype(jnp.int32)
    for k in range(batches):
        used = sizes_in[k]
        row = row_codes[k : k + 1]
        col = col_codes[:, k : k + 1]
        row = jnp.where(line[:1] < used, row, tiles * obs_tiles)
        col = jnp.where(down[:, :1] < used, col, tiles * obs_tiles)
        row_t, col_t = row // obs_tiles, col // obs_tiles
        same = row == col
        times = ones(same, 1)
        first_row = (ones(same & (down < line), 0) == 0) & (row_t < tiles)
        first_col = (ones(same & (line < down), 1) == 0) & (col_t < tiles)
        mates = row_t == col_t
        even_row = (ones(first_col & mates & (col < row), 0) & 1) == 0
        even_col = (ones(first_row & mates & (row < col), 1) & 1) == 0
        place = ones(first_row & even_row & (row <= col), 1) - 1
        here = first_col & (place == slot)
        value = ((col - col_t * obs_tiles) << 10) + times
        size = ones(first_row & even_row, 1)
        entry = jnp.sum(jnp.where(here & even_col, value + (col_t << 16), 0), axis=0, keepdims=True)
        other = jnp.sum(jnp.where(here & ~even_col, value, 0), axis=0, keepdims=True)
        lists[k : k + 1, :] = jnp.where(entry > 0, entry, tiles << 16)
        lists[batches + k : batches + k + 1, :] = jnp.where(slot[:1] == length - 1, size, other)


def pair_lists(pairs, counts, tiles, obs_tiles):
    batches, slots = pairs.shape[0], pairs.shape[2]
    length = -(-(slots + (AHEAD + 1) * GROUP) // 128) * 128
    return pl.pallas_call(
        functools.partial(list_kernel, tiles=tiles, obs_tiles=obs_tiles),
        out_shape=jax.ShapeDtypeStruct((2 * batches, length), jnp.int32),
        in_specs=[in_smem(), in_vmem()],
        out_specs=in_vmem(),
        cost_estimate=pl.CostEstimate(flops=40 * batches * slots * slots, bytes_accessed=16 * batches * slots, transcendentals=0),
        name="pair_lists",
    )(counts, pairs)


def feature_kernel(coord, feat, tall):
    tall[...] = cell_features(coord[...].astype(F32))
    for t in range(feat.shape[0]):
        feat[t] = tall[:, t * CT : (t + 1) * CT].T.astype(BF16)


def features(coord):
    cells = coord.shape[1]
    return pl.pallas_call(
        feature_kernel,
        out_shape=jax.ShapeDtypeStruct((cells // CT, CT, 16), BF16),
        in_specs=[in_vmem()],
        out_specs=in_vmem(),
        scratch_shapes=[pltpu.VMEM((16, cells), F32)],
        cost_estimate=pl.CostEstimate(flops=300 * cells, bytes_accessed=300 * cells, transcendentals=0),
        name="cell_features",
    )(coord)


def centre_kernel(state, work):
    members = state.shape[1]
    for t in range(work.shape[0]):
        x = state[t * CT : (t + 1) * CT, :].astype(F32)
        work[t, :, :members] = x
        work[t, :, members:] = x - jnp.mean(x, axis=1, keepdims=True)


def centred(state, first, tiles):
    members = state.shape[1]
    share = 4 if first % 4 == 0 and tiles % 4 == 0 else 1
    return pl.pallas_call(
        centre_kernel,
        out_shape=jax.ShapeDtypeStruct((tiles, CT, 2 * members), F32),
        grid=(tiles // share,),
        in_specs=[pl.BlockSpec((share * CT, members), lambda i: (i + first // share, 0))],
        out_specs=pl.BlockSpec((share, CT, 2 * members), lambda i: (i, 0, 0)),
        cost_estimate=pl.CostEstimate(
            flops=4 * tiles * CT * members, bytes_accessed=10 * tiles * CT * members, transcendentals=0
        ),
        name="centred_state",
    )(state)


def filter_kernel(lists, cell_lines, works, rest, *refs, pieces_count):
    pieces, out, scratch = refs[:pieces_count], refs[pieces_count], refs[pieces_count + 1 :]
    blocks, ys, wd, of, gs, us, both_ref, bt, mp, acc, pert, feat, held, final, walk, arrived, left = scratch
    batches, obs_tiles = of.shape[:2]
    tiles, _, members = pert.shape
    tiles -= 1
    several = 4 if tiles % 4 == 0 else 1

    copies = [pltpu.make_async_copy(piece, blocks.at[d], arrived.at[d]) for d, piece in enumerate(pieces)]
    cut = works.shape[0]
    moves = (
        (lists, walk),
        (cell_lines, feat.at[pl.ds(0, tiles)]),
        (works, acc.at[pl.ds(0, cut)]),
        (rest, acc.at[pl.ds(cut, tiles - cut)]),
    )
    for n, (source, target) in enumerate(moves):
        copies.append(pltpu.make_async_copy(source, target, arrived.at[pieces_count + n]))
    for copy in copies:
        copy.start()

    rows = lax.broadcasted_iota(jnp.int32, (members, members), 0)
    cols = lax.broadcasted_iota(jnp.int32, (members, members), 1)
    eye = jnp.where(rows == cols, 1.0, 0.0)
    my_tile, my_batch = lax.axis_index("cell"), lax.axis_index("dp")

    acc[tiles] = jnp.zeros((CT, 2 * members), F32)
    pert[tiles] = jnp.zeros((CT, members), BF16)
    feat[tiles] = jnp.zeros((CT, 16), BF16)

    def over_tiles(body):
        def some(i, _):
            for j in range(several):
                body(i * several + j)
            return 0

        lax.fori_loop(0, tiles // several, some, 0)

    for rd in range(batches):
        copies[rd].wait()
        lefts, rights = [], []
        k = my_batch ^ rd
        for rc in range(obs_tiles):
            u = my_tile ^ rc
            r = place_of(rc, obs_tiles)
            raw = blocks[rd, r, :members, :]
            y = raw.astype(F32)
            e = blocks[rd, r, members:, :].astype(F32)
            value = e[0:1] + e[1:2] + e[2:3]
            variance = e[3:4] + e[4:5] + e[5:6]
            mean = jnp.mean(y, axis=0, keepdims=True)
            w = 1.0 / variance
            where = pl.ds(pl.multiple_of(u * OBS_DEV, OBS_DEV), OBS_DEV)
            ys[k, :, where] = raw
            wd[k, 0:1, where] = w
            wd[k, 1:2, where] = value
            of[k, u] = obs_features(e[6:9])
            z = jnp.broadcast_to((value - mean) * w, (16, OBS_DEV))
            lefts.append(parts(jnp.concatenate([(y - mean) * w, z], axis=0)))
            rights.append(raw)
        right = jnp.concatenate(rights, axis=1)
        g = sum(
            lax.dot_general(
                jnp.concatenate(part, axis=1), right, (((1,), (1,)), ((), ())), preferred_element_type=F32
            )
            for part in zip(*lefts)
        )
        g = g - jnp.mean(g, axis=1, keepdims=True)
        gs[k] = g[:members]
        us[k] = g[members:]

    qt = eye - 1.0 / members
    p = jnp.full((16, members), 1.0 / members, F32)
    chunk = min(2, obs_tiles) * OBS_DEV
    series, scale = series_start(eye, gs[0] * (1.0 / (members - 1)))
    for _ in range(3):
        series = series_step(eye, series)
    for k in range(batches):
        inverse = scale * series_end(eye, series, both_ref)
        inverse_parts = parts(inverse)
        qt_parts = parts(qt)
        mt = mm_parts(inverse_parts, qt_parts)
        ht = 0.5 * qt + p[0:1]
        hi, mid, lo = parts(jnp.concatenate([mt, ht], axis=0))
        twice = jnp.concatenate([hi, mid], axis=1)
        for n in range(obs_tiles * OBS_DEV // chunk):
            where = pl.ds(n * chunk, chunk)
            y = ys[k, :, where]
            both = mm16(twice, jnp.concatenate([y, y], axis=0)) + mm16(lo, y)
            b = (both[:members] * (1.0 / (members - 1))).astype(BF16)
            pull = wd[k, 0:1, where] * (wd[k, 1:2, where] - both[members:])
            pulls = jnp.concatenate([pull, pull - jnp.mean(pull, axis=0, keepdims=True)], axis=0).astype(BF16)
            for c in range(chunk // OBS_DEV):
                u = n * (chunk // OBS_DEV) + c
                bt[u] = b[:, c * OBS_DEV : (c + 1) * OBS_DEV]
                mp[u] = pulls[:, c * OBS_DEV : (c + 1) * OBS_DEV].T
        if k + 1 < batches:
            half = parts(0.5 * (eye + inverse))
            step = parts(mm_parts(parts(us[k]), inverse_parts) * (1.0 / (members - 1)))
            p = p + mm_parts(step, qt_parts)
            qt = 0.5 * (qt + mt)

        def change_basis(j):
            g_j = parts(gs[j])
            gs[j] = mm_parts(half, parts(mm_parts(g_j, half)))
            us[j] = mm_parts(parts(us[j] - mm_parts(step, g_j)), half)

        if k == 0:
            for copy in copies[pieces_count:]:
                copy.wait()

        def centre(t):
            pert[t] = acc[t, :, members:].astype(BF16)

        over_tiles(centre)

        def named(i, j):
            e, o = walk[k, i * GROUP + j], walk[batches + k, i * GROUP + j]
            return e >> 16, (e >> 10) & 63, o >> 10, e & 1023, o & 1023

        def weigh(i):
            for j in range(GROUP):
                t, u0, u1, m0, m1 = named(i, j)
                score = mm16(pert[t], jnp.concatenate([bt[u0], bt[u1]], axis=1))
                power = mm16(feat[t], jnp.concatenate([of[k, u0], of[k, u1]], axis=1))
                taper = jnp.exp2(power)
                for n, m in enumerate((m0, m1)):
                    cut = slice(n * OBS_DEV, (n + 1) * OBS_DEV)
                    held[j, :, cut] = (taper[:, cut] * (score[:, cut] * m.astype(F32))).astype(BF16)

        def draw(i):
            for j in range(GROUP):
                t, u0, u1, _, _ = named(i, j)
                acc[t] += mm16(held[j], jnp.concatenate([mp[u0], mp[u1]], axis=0))

        def group(i, _):
            draw(i - 1)
            weigh(i)
            return 0

        groups = (walk[batches + k, walk.shape[1] - 1] + GROUP - 1) // GROUP
        weigh(0)
        if k + 1 < batches:
            change_basis(k + 1)
            for i in range(1, AHEAD):
                draw(i - 1)
                if i == 1:
                    series, scale = series_start(eye, gs[k + 1] * (1.0 / (members - 1)))
                else:
                    series = series_step(eye, series)
                if k + 1 + i < batches:
                    change_basis(k + 1 + i)
                weigh(i)
            groups = jnp.maximum(groups, AHEAD)
            lax.fori_loop(AHEAD, groups, group, 0)
        else:
            lax.fori_loop(1, groups, group, 0)
        draw(groups - 1)

    leaving = []
    for n in range(left.shape[0]):
        share = tiles // left.shape[0]

        def finish(i, _):
            t = n * share + i
            final[pl.ds(pl.multiple_of(t * CT, CT), CT), :] = acc[t, :, :members].astype(BF16)
            return 0

        lax.fori_loop(0, share, finish, 0)
        where = pl.ds(n * share * CT, share * CT)
        leaving.append(pltpu.make_async_copy(final.at[where], out.at[where], left.at[n]))
        leaving[-1].start()
    for copy in leaving:
        copy.wait()


def filtered(lists, cell_lines, works, pieces):
    batches = len(pieces)
    obs_tiles, rows = pieces[0].shape[:2]
    tiles = cell_lines.shape[0]
    members = works[0].shape[2] // 2
    cells = tiles * CT
    shares = 4 if tiles % 4 == 0 else 1
    anywhere = pl.BlockSpec(memory_space=pl.ANY)
    return pl.pallas_call(
        functools.partial(filter_kernel, pieces_count=batches),
        out_shape=jax.ShapeDtypeStruct((cells, members), BF16),
        in_specs=[anywhere] * (4 + batches),
        out_specs=anywhere,
        scratch_shapes=[
            pltpu.VMEM((batches, obs_tiles, rows, OBS_DEV), BF16),
            pltpu.VMEM((batches, members, obs_tiles * OBS_DEV), BF16),
            pltpu.VMEM((batches, 8, obs_tiles * OBS_DEV), F32),
            pltpu.VMEM((batches, obs_tiles, 16, OBS_DEV), BF16),
            pltpu.VMEM((batches, members, members), F32),
            pltpu.VMEM((batches, 16, members), F32),
            pltpu.VMEM((2 * members, members), F32),
            pltpu.VMEM((obs_tiles, members, OBS_DEV), BF16),
            pltpu.VMEM((obs_tiles, OBS_DEV, 2 * members), BF16),
            pltpu.VMEM((tiles + 1, CT, 2 * members), F32),
            pltpu.VMEM((tiles + 1, CT, members), BF16),
            pltpu.VMEM((tiles + 1, CT, 16), BF16),
            pltpu.VMEM((GROUP, CT, 2 * OBS_DEV), BF16),
            pltpu.VMEM((cells, members), BF16),
            pltpu.SMEM(lists.shape, jnp.int32),
            pltpu.SemaphoreType.DMA((batches + 4,)),
            pltpu.SemaphoreType.DMA((shares,)),
        ],
        compiler_params=pltpu.CompilerParams(vmem_limit_bytes=VMEM_LIMIT),
        name="filter",
    )(lists, cell_lines, *works, *pieces)


def local(
    state,
    cell_coordinate,
    member_predictions,
    measured_values,
    obs_error_variance,
    observation_coordinate,
    localization_tile_pairs,
    used_pair_count,
):
    obs_tiles = lax.axis_size("cell")
    batches = lax.axis_size("dp")
    tiles = state.shape[0] // CT
    mine = pack(member_predictions[0], measured_values, obs_error_variance, observation_coordinate[0])

    jobs = [
        (features, (cell_coordinate,)),
        (functools.partial(centred, first=0, tiles=tiles // 2), (state,)),
        (functools.partial(centred, first=tiles // 2, tiles=tiles - tiles // 2), (state,)),
        (
            functools.partial(pair_lists, tiles=tiles, obs_tiles=obs_tiles),
            (localization_tile_pairs[0], used_pair_count[0]),
        ),
    ]
    pieces, (cell_lines, works, rest, lists) = gathered(mine, jobs)
    return filtered(lists, cell_lines, (works, rest), pieces)


def solution(mesh):
    placed = (
        P(("cell", "dp"), None),
        P(None, ("cell", "dp")),
        P("dp", "cell", None),
        P("dp", "cell"),
        P("dp", "cell"),
        P("dp", None, "cell"),
        P(("cell", "dp"), None, None, None),
        P(("cell", "dp"), None),
    )
    return jax.shard_map(
        local, mesh=mesh, in_specs=placed, out_specs=P(("cell", "dp"), None), check_vma=False
    )
```
